256 devices in a mesh: dp: 16 (over x, y_hi, core), mp: 16 (over y_lo, z).
Axes of the slice: x: 4, y: 4 (y_hi: 2, y_lo: 2; y = y_hi * 2 + y_lo), z: 8, core: 2. Of those that a mesh axis runs over, the one named last changes fastest.
Arguments:
- acts: bfloat16 [4096, 8, 2048], P('dp', None, 'mp'), may hold values from -6 to 6
- cotangent: bfloat16 [4096, 8, 1024], P('dp'), may hold values from -0.09375 to 0.09375
- block_slot: int32 [8], replicated, may hold values from 0 to 31, as said below
- basis_in: bfloat16 [32, 2048, 2048], P('dp', None, 'mp'), may hold values from -0.125 to 0.125
- basis_out: bfloat16 [32, 1024, 1024], P('dp', 'mp'), may hold values from -0.1875 to 0.1875
- moment_first: float32 [32, 2048, 1024], P('dp', 'mp'), may hold values from -3 to 3
- moment_second: float32 [32, 2048, 1024], P('dp', 'mp'), may hold values from 0.05 to 2
Outputs:
- new_first: float32 [32, 2048, 1024], P('dp', 'mp')
- new_second: float32 [32, 2048, 1024], P('dp', 'mp')
- stat_in: float32 [32, 2048, 2048], P('dp', 'mp')
- update: bfloat16 [8, 2048, 1024], P(None, 'mp', 'dp')
The draws below stay inside these ranges and needn't reach their ends.
Inputs may be any that keep to these rules, and one draw needn't show every extreme that they name: `block_slot`: the values are distinct. Slot s belongs to preconditioner group s // 2; in every draw one group owns 2 blocks and every other group owns at most one.
All inputs are finite; a program needn't handle non-finite values.
Results may differ from the reference program's by a relative error of at most 0.03.
Values may be sent and summed in bfloat16 or wider, within the bound.
A program may use at most 128 MiB of HBM per device.

```python
import math
import jax
import jax.numpy as jnp
from jax import lax

BLK_IN = 2048
BLK_OUT = 1024
NBLK = 8
SLOTS = 2
TOK_DEV = 256
TOKENS = 4096
SLOT_TOTAL = 32
N_DP = 16
N_MP = 16


def draw_block_slot(key, part):
    key = jax.random.fold_in(key, 7)
    key_groups, key_order, key_chosen = jax.random.split(key, 3)
    shuffled = jax.random.permutation(key_groups, N_DP).astype(jnp.int32)
    final_group = N_DP - 1
    where_final = jnp.argmax(shuffled == final_group).astype(jnp.int32)
    runner_up = shuffled[1]
    swapped = shuffled.at[where_final].set(runner_up).at[1].set(final_group)
    arranged = jnp.where(where_final > 0, swapped, shuffled)
    busiest = arranged[0]
    position = jnp.arange(NBLK, dtype=jnp.int32)
    other_groups = arranged[jnp.clip(position - SLOTS + 1, 1, N_DP - 1)]
    chosen = jax.random.randint(key_chosen, (NBLK,), 0, SLOTS, dtype=jnp.int32)
    chosen = jnp.where(position == SLOTS, SLOTS - 1, chosen)
    slot_values = jnp.where(position < SLOTS, busiest * SLOTS + position, other_groups * SLOTS + chosen)
    ordering = jax.random.permutation(key_order, NBLK)
    return slot_values[ordering].astype(jnp.int32)


def levels(rng, extent, cuts, least, top_value):
    factor_of, own = 1.0, jax.random.fold_in(rng, 6)
    for dim, blocks in cuts:
        draws = jnp.exp(jax.random.uniform(jax.random.fold_in(own, dim), (blocks,), jnp.float32, least / len(cuts), top_value / len(cuts)))
        factor_of = factor_of * jnp.repeat(draws, extent[dim] // blocks).reshape([-1 if axis == dim else 1 for axis in range(len(extent))])
    return factor_of


def noise(key, extent, width, limit, pieces=(), held_as=jnp.bfloat16):
    entries = jax.random.normal(key, extent, jnp.float32) * width
    if len(pieces) > 0:
        entries = levels(key, extent, pieces, -0.22, 0.18) * entries
    return jnp.clip(entries, min=-limit, max=limit).astype(held_as)


def setup_inputs(seed: int = 0) -> dict:
    streams_of = jax.random.split(jax.random.key(seed), 8)
    return {
        "acts": noise(streams_of[0], (TOKENS, NBLK, BLK_IN), 1.0, 6.0, ((0, 16), (2, 16))),
        "cotangent": noise(streams_of[1], (TOKENS, NBLK, BLK_OUT), (1.0 / TOKENS ** 0.5), 0.09375, ((0, 16),)),
        "block_slot": draw_block_slot(jax.random.fold_in(streams_of[7], 71), 0),
        "basis_in": noise(streams_of[3], (SLOT_TOTAL, BLK_IN, BLK_IN), BLK_IN ** -0.5, 0.125, ((0, 16), (2, 16))),
        "basis_out": noise(streams_of[4], (SLOT_TOTAL, BLK_OUT, BLK_OUT), BLK_OUT ** -0.5, 0.1875, ((0, 16), (1, 16))),
        "moment_first": noise(streams_of[5], (SLOT_TOTAL, BLK_IN, BLK_OUT), 0.5, 3.0, ((0, 16), (1, 16)), jnp.float32),
        "moment_second": jnp.clip(jnp.exp(math.log(2.0) - 3.6888794 * jax.random.uniform(streams_of[6], (SLOT_TOTAL, BLK_IN, BLK_OUT), jnp.float32) ** levels(streams_of[6], (SLOT_TOTAL, BLK_IN, BLK_OUT), ((0, 16), (1, 16)), -0.2, 0.2)), 0.05, 2.0),
    }


def reference(acts, cotangent, block_slot, basis_in, basis_out, moment_first, moment_second):
    group_rows = BLK_IN // N_MP

    def one_block(block_index):
        slot_index = block_slot[block_index]
        inputs_b = lax.dynamic_index_in_dim(acts, block_index, 1, keepdims=False)
        grads_out = lax.dynamic_index_in_dim(cotangent, block_index, 1, keepdims=False)
        inputs_b = inputs_b.reshape(N_DP, TOK_DEV, BLK_IN).astype(jnp.float32)
        grads_out = grads_out.reshape(N_DP, TOK_DEV, BLK_OUT).astype(jnp.float32)
        learner_parts = jnp.einsum('gti,gto->gio', inputs_b, grads_out).astype(jnp.bfloat16)
        learner_parts = lax.optimization_barrier(learner_parts)
        grad = lax.optimization_barrier(jnp.sum(learner_parts.astype(jnp.float32), axis=0))
        grad_block = grad.astype(jnp.bfloat16)
        left_basis = lax.dynamic_index_in_dim(basis_in, slot_index, 0, keepdims=False)
        right_basis = lax.dynamic_index_in_dim(basis_out, slot_index, 0, keepdims=False)
        statistic = jnp.dot(grad_block, grad_block.T, preferred_element_type=jnp.float32)
        left_rotated = jnp.dot(left_basis.T, grad_block, preferred_element_type=jnp.float32).astype(jnp.bfloat16)
        rotated = jnp.dot(left_rotated, right_basis, preferred_element_type=jnp.float32)
        first_old = lax.dynamic_index_in_dim(moment_first, slot_index, 0, keepdims=False)
        second_old = lax.dynamic_index_in_dim(moment_second, slot_index, 0, keepdims=False)
        first_new = 0.9 * first_old + 0.1 * rotated
        second_new = 0.95 * second_old + 0.05 * rotated * rotated
        direction = (first_new / jnp.sqrt(second_new)).astype(jnp.bfloat16)
        back_rotated = jnp.dot(direction, right_basis.T, preferred_element_type=jnp.float32).astype(jnp.bfloat16)
        basis_groups = left_basis.reshape(BLK_IN, N_MP, group_rows).astype(jnp.float32)
        back_groups = back_rotated.reshape(N_MP, group_rows, BLK_OUT).astype(jnp.float32)
        group_parts = jnp.einsum('igr,gro->gio', basis_groups, back_groups).astype(jnp.bfloat16)
        group_parts = lax.optimization_barrier(group_parts)
        update_block = lax.optimization_barrier(jnp.sum(group_parts.astype(jnp.float32), axis=0)).astype(jnp.bfloat16)
        return (rotated, statistic, update_block)
    rotated_blocks, stat_blocks, update = lax.map(one_block, jnp.arange(NBLK, dtype=jnp.int32))
    slot_count = basis_in.shape[0]
    rotated_all = jnp.zeros((slot_count, BLK_IN, BLK_OUT), jnp.float32).at[block_slot].set(rotated_blocks)
    stat_in = jnp.zeros((slot_count, BLK_IN, BLK_IN), jnp.float32).at[block_slot].set(stat_blocks)
    new_first = 0.9 * moment_first + 0.1 * rotated_all
    new_second = 0.95 * moment_second + 0.05 * rotated_all * rotated_all
    return (new_first, new_second, stat_in, update)
```

```python
import functools

import jax
import jax.numpy as jnp
from jax import lax
from jax.experimental import pallas as pl
from jax.experimental.pallas import tpu as pltpu
from jax.sharding import PartitionSpec as P

MESH = pl.DeviceIdType.MESH
BF = jnp.bfloat16
F32 = jnp.float32
NX, NZ = 4, 8
NB = 8


def nt(a, b):
    return lax.dot_general(a, b, (((1,), (1,)), ((), ())), preferred_element_type=F32)


def nn(a, b):
    return jnp.dot(a, b, preferred_element_type=F32)


def tn(a, b):
    return lax.dot_general(a, b, (((0,), (0,)), ((), ())), preferred_element_type=F32)


class Net:
    def __init__(self, ssem, rsem):
        self.ssem, self.rsem, self.used, self.sent = ssem, rsem, 0, []
        dp, mp = lax.axis_index("dp"), lax.axis_index("mp")
        self.x, self.yh, self.c = dp // 4, (dp // 2) % 2, dp % 2
        self.yl, self.z = mp // NZ, mp % NZ

    def at(self, x=None, yh=None, c=None, yl=None, z=None):
        x = self.x if x is None else x
        yh = self.yh if yh is None else yh
        c = self.c if c is None else c
        yl = self.yl if yl is None else yl
        z = self.z if z is None else z
        return (x * 4 + yh * 2 + c, yl * NZ + z)

    def send(self, src, dst, device):
        i = self.used
        self.used += 1
        copy = pltpu.make_async_remote_copy(
            src_ref=src,
            dst_ref=dst,
            send_sem=self.ssem.at[i],
            recv_sem=self.rsem.at[i],
            device_id=device,
            device_id_type=MESH,
        )
        copy.start()
        self.sent.append(copy)
        return copy

    def drain(self):
        for copy in self.sent:
            copy.wait_send()

    def mate(self, src, dst):
        return self.send(src, dst, self.at(c=1 - self.c))

    def xs(self):
        return [lax.rem(self.x + k, NX) for k in (1, 2, 3)]


class Scatter:
    def __init__(self, net, t, bufs, out, kind, step):
        self.net, self.t, self.out, self.kind, self.step = net, t, out, kind, step
        self.x0, self.y0, self.y1, self.x1 = bufs
        self.rows = t.shape[2]
        self.half = self.rows // 2

    def start(self):
        net, h = self.net, self.half
        self.cy1 = net.send(
            self.t.at[:, 1 - net.yh, pl.ds(h, h), :], self.y1, net.at(yh=1 - net.yh)
        )
        self.cx0 = [
            net.send(self.t.at[xp, :, pl.ds(0, h), :], self.x0.at[k], net.at(x=xp))
            for k, xp in enumerate(net.xs())
        ]

    def add(self, dst, srcs):
        total = None
        n, kind = self.step, self.kind

        def body(i, carry):
            rows = pl.ds(pl.multiple_of(i * n, n), n)
            total = None
            for src in srcs:
                part = src(rows).astype(kind)
                total = part if total is None else total + part
            dst(rows, total.astype(BF))
            return carry

        del total
        lax.fori_loop(0, self.half // n, body, 0)

    def rows_of(self, ref, base=0):
        def load(rows):
            return ref[pl.ds(pl.multiple_of(rows.start + base, 16), rows.size), :]

        return load

    def store_of(self, ref, base=0):
        def store(rows, value):
            ref[pl.ds(pl.multiple_of(rows.start + base, 16), rows.size), :] = value

        return store

    def middle(self):
        net, h, t = self.net, self.half, self.t
        for copy in self.cx0:
            copy.wait_recv()
        for yp in (1 - net.yh, net.yh):
            mine = t.at[net.x, yp]
            self.add(
                self.store_of(mine),
                [self.rows_of(mine)] + [self.rows_of(self.x0.at[k, yp]) for k in range(3)],
            )
            if yp is not net.yh:
                self.cy0 = net.send(
                    t.at[net.x, 1 - net.yh, pl.ds(0, h), :], self.y0, net.at(yh=1 - net.yh)
                )
        self.cy1.wait_recv()
        self.cx1 = []
        for k, xp in enumerate(net.xs() + [net.x]):
            mine = t.at[xp, net.yh]
            self.add(self.store_of(mine, h), [self.rows_of(mine, h), self.rows_of(self.y1.at[xp])])
            if k < 3:
                self.cx1.append(
                    net.send(t.at[xp, net.yh, pl.ds(h, h), :], self.x1.at[k], net.at(x=xp))
                )

    def finish(self):
        net, h = self.net, self.half
        mine = self.t.at[net.x, net.yh]
        self.cy0.wait_recv()
        self.add(self.store_of(self.out), [self.rows_of(mine), self.rows_of(self.y0)])
        for copy in self.cx1:
            copy.wait_recv()
        self.add(
            self.store_of(self.out, h),
            [self.rows_of(mine, h)] + [self.rows_of(self.x1.at[k]) for k in range(3)],
        )


class Spread:
    def __init__(self, net, a):
        self.net, self.a, self.half = net, a, a.shape[2] // 2

    def start(self):
        net, h, a = self.net, self.half, self.a
        last = a.at[net.x, net.yh, pl.ds(h, h), :]
        self.cy = net.send(last, last, net.at(yh=1 - net.yh))
        first = a.at[net.x, net.yh, pl.ds(0, h), :]
        self.cx = [net.send(first, first, net.at(x=xp)) for xp in net.xs()]

    def middle(self):
        net, h, a = self.net, self.half, self.a
        self.cy.wait_recv()
        last = a.at[net.x, :, pl.ds(h, h), :]
        self.cx2 = [net.send(last, last, net.at(x=xp)) for xp in net.xs()]
        for copy in self.cx:
            copy.wait_recv()
        first = a.at[:, net.yh, pl.ds(0, h), :]
        self.cy2 = net.send(first, first, net.at(yh=1 - net.yh))

    def finish(self):
        for copy in self.cx2:
            copy.wait_recv()
        self.cy2.wait_recv()


class Ring:
    def __init__(self, net, block):
        self.net, self.block = net, block
        self.up, self.down = {}, {}

    def hop(self, way, step, line):
        net = self.net
        yl = net.yl if line == 0 else 1 - net.yl
        sign = 1 if way == 0 else -1
        ref = self.block(yl, lax.rem(net.z - sign * step + NZ, NZ))
        copy = net.send(ref, ref, net.at(z=lax.rem(net.z + sign + NZ, NZ)))
        (self.up if way == 0 else self.down)[step, line] = copy

    def start(self):
        net = self.net
        own = self.block(net.yl, net.z)
        self.hop(0, 0, 0)
        self.hop(1, 0, 0)
        self.cy = net.send(own, own, net.at(yl=1 - net.yl))

    def step(self, s):
        if s == 0:
            self.cy.wait_recv()
            self.hop(0, 0, 1)
            self.hop(1, 0, 1)
            return
        for line in (0, 1):
            self.up[s - 1, line].wait_recv()
            if s < 3 or line == 0:
                self.hop(0, s, line)
            self.down[s - 1, line].wait_recv()
            if s < 3 or line == 1:
                self.hop(1, s, line)

    def finish(self):
        self.up[3, 0].wait_recv()
        self.down[3, 1].wait_recv()


def kernel(
    slot_ref, p_ref, b_ref, o_ref, m1_ref, m2_ref, r_out, s_out, u_out,
    prec, tg, gx0, gy0, gy1, gx1,
    cb, tb, bx0, by0, by1, bx1, bfull,
    co, to, ox0, oy0, oy1, ox1, ofin, oall,
    mb, cm, tm, mx0, my0, my1, mx1, mfin,
    gall, lfull, lacc, stat, smate, dfull, kbuf,
    rall, rpick, rmate, sall, spick, sgot,
    usend, urecv, ylsend, ylrecv, ufin, uall,
    ssem, rsem, asend, arecv,
):
    net = Net(ssem, rsem)
    x, yh, c, yl, z = net.x, net.yh, net.c, net.yl, net.z
    dp = lax.axis_index("dp")
    home = x * 2 + yh
    oc = 1 - c

    barrier = pltpu.get_barrier_semaphore()
    others = [
        net.at(x=lax.rem(x + i, NX), yh=lax.rem(yh + j, 2), c=lax.rem(c + k, 2))
        for i in range(4) for j in range(2) for k in range(2) if (i, j, k) != (0, 0, 0)
    ]
    others += [net.at(yl=1 - yl), net.at(z=lax.rem(z + 1, NZ)), net.at(z=lax.rem(z + NZ - 1, NZ))]
    for device in others:
        pl.semaphore_signal(barrier, inc=1, device_id=device, device_id_type=MESH)

    def pick(b):
        local = slot_ref[b] - (dp - c) * 2
        inside = (local >= 0) & (local < 4)
        return jnp.where(inside, lax.rem(local + 2 * c + 4, 4), 4)

    def block_of(group, s):
        found = 8
        for b in range(NB):
            found = jnp.where(slot_ref[b] == group * 2 + s, b, found)
        return found

    half_lanes = pl.ds(pl.multiple_of(c * 512, 512), 512)
    other_lanes = pl.ds(pl.multiple_of(oc * 512, 512), 512)
    half_b = pl.ds(pl.multiple_of(c * 1024, 1024), 1024)
    other_b = pl.ds(pl.multiple_of(oc * 1024, 1024), 1024)
    half_o = pl.ds(pl.multiple_of(c * 32, 32), 32)
    other_o = pl.ds(pl.multiple_of(oc * 32, 32), 32)

    for s in range(2):
        mb[s, 0:128, :] = m1_ref[s].astype(BF)
        mb[s, 128:256, :] = m2_ref[s].astype(BF)
    pl.semaphore_wait(barrier, len(others))

    pcopies = [
        net.mate(p_ref.at[pl.ds(i * 4, 4), :, other_lanes], prec.at[pl.ds(i * 4, 4)]) for i in range(2)
    ]
    bcopy = net.mate(b_ref.at[:, other_b, :], cb.at[pl.ds(2, 2)])
    ocopy = net.mate(o_ref.at[:, other_o, :], co.at[pl.ds(2, 2)])
    mcopy = net.mate(mb.at[:, :, other_lanes], cm.at[pl.ds(2, 2)])

    for i in range(2):
        pcopies[i].wait_recv()

        def add_cores(b, carry):
            total = p_ref[b, :, half_lanes].astype(F32) + prec[b].astype(F32)
            tg[b // 2, b % 2] = total.astype(BF)
            return carry

        lax.fori_loop(i * 4, i * 4 + 4, add_cores, 0)
    grads = Scatter(net, tg, (gx0, gy0, gy1, gx1), gall.at[yl, z], F32, 32)
    grads.start()

    for s in range(2):
        cb[s] = b_ref[s, half_b, :]
        co[s] = o_ref[s, half_o, :]
        cm[s] = mb[s, :, half_lanes]
    cb[4] = jnp.zeros_like(cb[4])
    co[4] = jnp.zeros_like(co[4])
    cm[4] = jnp.zeros_like(cm[4])
    bcopy.wait_recv()
    ocopy.wait_recv()
    mcopy.wait_recv()

    def choose(b, carry):
        i = pick(b)
        tb[b // 2, b % 2] = cb[i]
        to[b // 2, b % 2] = co[i]
        tm[b // 2, b % 2] = cm[i]
        return carry

    lax.fori_loop(0, NB, choose, 0)

    grads.middle()
    half16 = pl.ds(pl.multiple_of(c * 8, 8), 8)
    left = Scatter(net, tb, (bx0, by0, by1, bx1), None, BF, 128)
    right = Scatter(net, to, (ox0, oy0, oy1, ox1), oall.at[yl, z, c], BF, 16)
    moments = Scatter(net, tm, (mx0, my0, my1, mx1), mfin, BF, 32)
    left.out = bfull.at[half_b]
    left.start()
    right.start()
    grads.finish()

    gring = Ring(net, lambda a, b: gall.at[a, b])
    gring.start()
    gring.step(0)
    gring.step(1)
    left.middle()
    gring.step(2)
    right.middle()
    moments.start()
    gring.step(3)
    left.finish()
    bmate = net.mate(bfull.at[half_b], bfull.at[half_b])
    right.finish()
    oring = Ring(net, lambda a, b: oall.at[a, b, c])
    oring.start()
    oring.step(0)
    gring.finish()
    bmate.wait_recv()

    lacc[...] = jnp.zeros_like(lacc)
    mine = gall.at[yl, z]

    def rows_step(i, carry):
        part = gall[i // NZ, i % NZ]
        at = pl.multiple_of(i * 128, 128)
        lacc[...] += tn(bfull[pl.ds(at, 128), :], part)
        stat[:, pl.ds(at, 128)] = nt(mine[...], part)
        return carry

    lax.fori_loop(0, 16, rows_step, 0)
    lfull[:, half_lanes] = lacc[...].astype(BF)
    lmate = net.mate(lfull.at[:, half_lanes], lfull.at[:, half_lanes])
    mine_s = pl.ds(pl.multiple_of(c * 64, 64), 64)
    other_s = pl.ds(pl.multiple_of(oc * 64, 64), 64)
    cstat = net.mate(stat.at[other_s, :], smate)

    oring.step(1)
    moments.middle()
    oring.step(2)
    oring.step(3)
    oring.finish()
    omate = net.mate(oall.at[:, :, c], oall.at[:, :, c])
    cstat.wait_recv()
    sall[x, yh] = (stat[mine_s, :] + smate[...]).astype(BF)
    lmate.wait_recv()
    omate.wait_recv()

    basis = oall[:, :, :, :, half_lanes].reshape(1024, 512)
    rotated = nn(lfull[...], basis)
    rall[x, yh] = rotated.astype(BF)
    moments.finish()
    rspread = Spread(net, rall)
    rspread.start()
    first = 0.9 * mfin[0:128, :].astype(F32) + 0.1 * rotated
    second = 0.95 * mfin[128:256, :].astype(F32) + 0.05 * rotated * rotated
    dfull[:, half_lanes] = (first / jnp.sqrt(second)).astype(BF)
    dmate = net.mate(dfull.at[:, half_lanes], dfull.at[:, half_lanes])
    dmate.wait_recv()
    kbuf[...] = nt(dfull[...], oall[c].reshape(512, 1024)).astype(BF)

    sspread = Spread(net, sall)
    sspread.start()

    def part(zd, yd):
        at = pl.multiple_of((yd * NZ + zd) * 128, 128)
        return nn(bfull[pl.ds(at, 128), :], kbuf[...])

    hops = {}

    def ring_hop(way, s, yd):
        sign = 1 if way == 0 else -1
        value = part(lax.rem(z + sign * (4 - s) + NZ, NZ), yd)
        if (way, s - 1, yd) in hops:
            hops[way, s - 1, yd].wait_recv()
            value = value + urecv[way, s - 1, yd].astype(F32)
        usend[way, s, yd] = value.astype(BF)
        hops[way, s, yd] = net.send(
            usend.at[way, s, yd], urecv.at[way, s, yd], net.at(z=lax.rem(z + sign + NZ, NZ))
        )

    def ring_step(s):
        for yd in (0, 1):
            for way in (0, 1):
                if s > 0 or way == yd:
                    ring_hop(way, s, yd)

    ring_step(0)
    ring_step(1)
    rspread.middle()
    ring_step(2)
    sspread.middle()
    ring_step(3)

    rspread.finish()
    zero_r = jnp.zeros((128, 512), BF)
    zero_s = jnp.zeros((64, 2048), BF)

    def chosen(ref, zero, group, s):
        b = block_of(group, s)
        b0 = jnp.minimum(b, NB - 1)
        return jnp.where(b < NB, ref[b0 // 2, b0 % 2], zero)

    mate_group = dp - c + oc
    for s in range(2):
        rpick[s] = chosen(rall, zero_r, mate_group, s)
    crm = net.mate(rpick, rmate)

    for way in (0, 1):
        for yd in (0, 1):
            hops[way, 3, yd].wait_recv()

    def final(yd):
        return part(z, yd) + urecv[0, 3, yd].astype(F32) + urecv[1, 3, yd].astype(F32)

    ylsend[...] = final(1 - yl).astype(BF)
    cyl = net.send(ylsend, ylrecv, net.at(yl=1 - yl))
    own = final(yl)
    sspread.finish()
    for s in range(2):
        spick[s] = chosen(sall, zero_s, mate_group, s)
    csm = net.mate(spick, sgot)
    cyl.wait_recv()
    ufin[...] = (own + ylrecv[...].astype(F32)).astype(BF)

    def to_columns(j, k):
        tx, ty = 2 * c + j // 2, j % 2
        here = (tx == x) & (ty == yh) & (k == c)
        src = ufin.at[:, pl.ds(j * 128, 128)]

        def copy():
            return pltpu.make_async_remote_copy(
                src_ref=src,
                dst_ref=uall.at[home],
                send_sem=asend.at[j * 2 + k],
                recv_sem=arecv.at[home],
                device_id=net.at(x=tx, yh=ty, c=k),
                device_id_type=MESH,
            )

        return here, copy

    for j in range(4):
        for k in range(2):
            here, copy = to_columns(j, k)

            @pl.when(jnp.logical_not(here))
            def _(copy=copy):
                copy().start()

            @pl.when(here)
            def _(j=j):
                uall[home] = ufin[:, j * 128 : (j + 1) * 128]

    for s in range(2):
        r_out[s, :, half_lanes] = chosen(rall, zero_r, dp, s)
        s_out[s, mine_s, :] = chosen(sall, zero_s, dp, s)
    crm.wait_recv()
    csm.wait_recv()
    for s in range(2):
        r_out[s, :, other_lanes] = rmate[s]
        s_out[s, other_s, :] = sgot[s]

    for b in range(NB):

        @pl.when(jnp.logical_not((b == home) & (c == x // 2)))
        def _(b=b):
            pltpu.make_async_remote_copy(
                src_ref=uall.at[b],
                dst_ref=uall.at[b],
                send_sem=asend.at[0],
                recv_sem=arecv.at[b],
                device_id=net.at(c=oc),
                device_id_type=MESH,
            ).wait_recv()

        value = uall[b]
        u_out[b] = jnp.where(c == 0, value[:, 0:64], value[:, 64:128])

    net.drain()
    for j in range(4):
        for k in range(2):
            here, copy = to_columns(j, k)

            @pl.when(jnp.logical_not(here))
            def _(copy=copy):
                copy().wait_send()


def scatter_bufs(rows, lanes):
    h = rows // 2
    return [
        pltpu.VMEM((4, 2, rows, lanes), BF),
        pltpu.VMEM((3, 2, h, lanes), BF),
        pltpu.VMEM((h, lanes), BF),
        pltpu.VMEM((4, h, lanes), BF),
        pltpu.VMEM((3, h, lanes), BF),
    ]


def step(block_slot, learner, basis_in, basis_out, moment_first, moment_second):
    vmem = pl.BlockSpec(memory_space=pltpu.VMEM)
    scratch = (
        [pltpu.VMEM((8, 128, 512), BF)] + scatter_bufs(128, 512)
        + [pltpu.VMEM((5, 1024, 128), BF)] + scatter_bufs(1024, 128) + [pltpu.VMEM((2048, 128), BF)]
        + [pltpu.VMEM((5, 32, 1024), BF)] + scatter_bufs(32, 1024)
        + [pltpu.VMEM((8, 128), BF), pltpu.VMEM((2, 8, 2, 32, 1024), BF)]
        + [pltpu.VMEM((2, 256, 1024), BF), pltpu.VMEM((5, 256, 512), BF)] + scatter_bufs(256, 512)
        + [pltpu.VMEM((256, 512), BF)]
        + [
            pltpu.VMEM((2, 8, 128, 512), BF),
            pltpu.VMEM((128, 1024), BF),
            pltpu.VMEM((128, 512), F32),
            pltpu.VMEM((128, 2048), F32),
            pltpu.VMEM((64, 2048), F32),
            pltpu.VMEM((128, 1024), BF),
            pltpu.VMEM((128, 512), BF),
            pltpu.VMEM((4, 2, 128, 512), BF),
            pltpu.VMEM((2, 128, 512), BF),
            pltpu.VMEM((2, 128, 512), BF),
            pltpu.VMEM((4, 2, 64, 2048), BF),
            pltpu.VMEM((2, 64, 2048), BF),
            pltpu.VMEM((2, 64, 2048), BF),
            pltpu.VMEM((2, 4, 2, 128, 512), BF),
            pltpu.VMEM((2, 4, 2, 128, 512), BF),
            pltpu.VMEM((128, 512), BF),
            pltpu.VMEM((128, 512), BF),
            pltpu.VMEM((128, 512), BF),
            pltpu.VMEM((8, 128, 128), BF),
            pltpu.SemaphoreType.DMA((128,)),
            pltpu.SemaphoreType.DMA((128,)),
            pltpu.SemaphoreType.DMA((8,)),
            pltpu.SemaphoreType.DMA((8,)),
        ]
    )
    return pl.pallas_call(
        kernel,
        out_shape=(
            jax.ShapeDtypeStruct((2, 128, 1024), BF),
            jax.ShapeDtypeStruct((2, 128, 2048), BF),
            jax.ShapeDtypeStruct((8, 128, 64), BF),
        ),
        in_specs=[pl.BlockSpec(memory_space=pltpu.SMEM)] + [vmem] * 5,
        out_specs=(vmem, vmem, vmem),
        scratch_shapes=scratch,
        compiler_params=pltpu.CompilerParams(
            collective_id=0, has_side_effects=True, vmem_limit_bytes=56 << 20
        ),
        name="soap_step",
    )(block_slot, learner, basis_in, basis_out, moment_first, moment_second)


def per_device(acts, cotangent, block_slot, basis_in, basis_out, moment_first, moment_second):
    learner = jnp.einsum("tbr,tbo->bro", acts, cotangent, preferred_element_type=F32).astype(BF)
    rotated, stat, update = step(block_slot, learner, basis_in, basis_out, moment_first, moment_second)
    rotated = rotated.astype(F32)
    new_first = 0.9 * moment_first + 0.1 * rotated
    new_second = 0.95 * moment_second + 0.05 * rotated * rotated
    return (new_first, new_second, stat.astype(F32), update)


def solution(mesh):
    placed = (
        P("dp", None, "mp"),
        P("dp", None, None),
        P(),
        P("dp", None, "mp"),
        P("dp", "mp", None),
        P("dp", "mp", None),
        P("dp", "mp", None),
    )
    return jax.shard_map(
        per_device,
        mesh=mesh,
        in_specs=placed,
        out_specs=(
            P("dp", "mp", None),
            P("dp", "mp", None),
            P("dp", "mp", None),
            P(None, "mp", "dp"),
        ),
        check_vma=False,
    )
```

```python
import functools

import jax
import jax.numpy as jnp
from jax import lax
from jax.experimental import pallas as pl
from jax.experimental.pallas import tpu as pltpu
from jax.sharding import PartitionSpec as P

MESH = pl.DeviceIdType.MESH
BF = jnp.bfloat16
F32 = jnp.float32
NX, NZ = 4, 8
NB = 8


def nt(a, b):
    return lax.dot_general(a, b, (((1,), (1,)), ((), ())), preferred_element_type=F32)


def nn(a, b):
    return jnp.dot(a, b, preferred_element_type=F32)


def tn(a, b):
    return lax.dot_general(a, b, (((0,), (0,)), ((), ())), preferred_element_type=F32)


class Net:
    def __init__(self, ssem, rsem):
        self.ssem, self.rsem, self.used, self.sent = ssem, rsem, 0, []
        dp, mp = lax.axis_index("dp"), lax.axis_index("mp")
        self.x, self.yh, self.c = dp // 4, (dp // 2) % 2, dp % 2
        self.yl, self.z = mp // NZ, mp % NZ

    def at(self, x=None, yh=None, c=None, yl=None, z=None):
        x = self.x if x is None else x
        yh = self.yh if yh is None else yh
        c = self.c if c is None else c
        yl = self.yl if yl is None else yl
        z = self.z if z is None else z
        return (x * 4 + yh * 2 + c, yl * NZ + z)

    def send(self, src, dst, device):
        i = self.used
        self.used += 1
        copy = pltpu.make_async_remote_copy(
            src_ref=src,
            dst_ref=dst,
            send_sem=self.ssem.at[i],
            recv_sem=self.rsem.at[i],
            device_id=device,
            device_id_type=MESH,
        )
        copy.start()
        self.sent.append(copy)
        return copy

    def drain(self):
        for copy in self.sent:
            copy.wait_send()

    def mate(self, src, dst):
        return self.send(src, dst, self.at(c=1 - self.c))

    def xs(self):
        return [lax.rem(self.x + k, NX) for k in (1, 2, 3)]


class Scatter:
    def __init__(self, net, t, bufs, out, kind, step):
        self.net, self.t, self.out, self.kind, self.step = net, t, out, kind, step
        self.x0, self.y0, self.y1, self.x1 = bufs
        self.rows = t.shape[2]
        self.half = self.rows // 2

    def start_x(self):
        net, h = self.net, self.half
        self.cx0 = [
            net.send(self.t.at[xp, :, pl.ds(0, h), :], self.x0.at[k], net.at(x=xp))
            for k, xp in enumerate(net.xs())
        ]

    def start_y(self):
        net, h = self.net, self.half
        self.cy1 = net.send(
            self.t.at[:, 1 - net.yh, pl.ds(h, h), :], self.y1, net.at(yh=1 - net.yh)
        )

    def start(self):
        self.start_y()
        self.start_x()

    def add(self, dst, srcs):
        total = None
        n, kind = self.step, self.kind

        def body(i, carry):
            rows = pl.ds(pl.multiple_of(i * n, n), n)
            total = None
            for src in srcs:
                part = src(rows).astype(kind)
                total = part if total is None else total + part
            dst(rows, total.astype(BF))
            return carry

        del total
        lax.fori_loop(0, self.half // n, body, 0)

    def rows_of(self, ref, base=0):
        def load(rows):
            return ref[pl.ds(pl.multiple_of(rows.start + base, 16), rows.size), :]

        return load

    def store_of(self, ref, base=0):
        def store(rows, value):
            ref[pl.ds(pl.multiple_of(rows.start + base, 16), rows.size), :] = value

        return store

    def middle(self):
        net, h, t = self.net, self.half, self.t
        for copy in self.cx0:
            copy.wait_recv()
        for yp in (1 - net.yh, net.yh):
            mine = t.at[net.x, yp]
            self.add(
                self.store_of(mine),
                [self.rows_of(mine)] + [self.rows_of(self.x0.at[k, yp]) for k in range(3)],
            )
            if yp is not net.yh:
                self.cy0 = net.send(
                    t.at[net.x, 1 - net.yh, pl.ds(0, h), :], self.y0, net.at(yh=1 - net.yh)
                )
        self.cy1.wait_recv()
        self.cx1 = []
        for k, xp in enumerate(net.xs() + [net.x]):
            mine = t.at[xp, net.yh]
            self.add(self.store_of(mine, h), [self.rows_of(mine, h), self.rows_of(self.y1.at[xp])])
            if k < 3:
                self.cx1.append(
                    net.send(t.at[xp, net.yh, pl.ds(h, h), :], self.x1.at[k], net.at(x=xp))
                )

    def finish(self):
        net, h = self.net, self.half
        mine = self.t.at[net.x, net.yh]
        self.cy0.wait_recv()
        self.add(self.store_of(self.out), [self.rows_of(mine), self.rows_of(self.y0)])
        for copy in self.cx1:
            copy.wait_recv()
        self.add(
            self.store_of(self.out, h),
            [self.rows_of(mine, h)] + [self.rows_of(self.x1.at[k]) for k in range(3)],
        )


class Spread:
    def __init__(self, net, a):
        self.net, self.a, self.half = net, a, a.shape[2] // 2

    def start(self):
        net, h, a = self.net, self.half, self.a
        last = a.at[net.x, net.yh, pl.ds(h, h), :]
        self.cy = net.send(last, last, net.at(yh=1 - net.yh))
        first = a.at[net.x, net.yh, pl.ds(0, h), :]
        self.cx = [net.send(first, first, net.at(x=xp)) for xp in net.xs()]

    def middle(self):
        net, h, a = self.net, self.half, self.a
        self.cy.wait_recv()
        last = a.at[net.x, :, pl.ds(h, h), :]
        self.cx2 = [net.send(last, last, net.at(x=xp)) for xp in net.xs()]
        for copy in self.cx:
            copy.wait_recv()
        first = a.at[:, net.yh, pl.ds(0, h), :]
        self.cy2 = net.send(first, first, net.at(yh=1 - net.yh))

    def finish(self):
        for copy in self.cx2:
            copy.wait_recv()
        self.cy2.wait_recv()


class Ring:
    def __init__(self, net, block, seen):
        self.net, self.block, self.seen = net, block, seen
        self.up, self.down = {}, {}

    def hop(self, way, step, line):
        net = self.net
        yl = net.yl if line == 0 else 1 - net.yl
        sign = 1 if way == 0 else -1
        ref = self.block(yl, lax.rem(net.z - sign * step + NZ, NZ))
        copy = net.send(ref, ref, net.at(z=lax.rem(net.z + sign + NZ, NZ)))
        (self.up if way == 0 else self.down)[step, line] = copy

    def start(self):
        net = self.net
        own = self.block(net.yl, net.z)
        self.hop(0, 0, 0)
        self.hop(1, 0, 0)
        self.cy = net.send(own, own, net.at(yl=1 - net.yl))
        self.seen(net.yl, net.z)

    def line(self, line, s):
        net = self.net
        yl = net.yl if line == 0 else 1 - net.yl
        if s == 0:
            self.cy.wait_recv()
            self.hop(0, 0, 1)
            self.hop(1, 0, 1)
            self.seen(yl, net.z)
            return
        self.up[s - 1, line].wait_recv()
        if s < 3 or line == 0:
            self.hop(0, s, line)
        self.down[s - 1, line].wait_recv()
        if s < 3 or line == 1:
            self.hop(1, s, line)
        self.seen(yl, lax.rem(net.z - s + NZ, NZ))
        self.seen(yl, lax.rem(net.z + s, NZ))

    def own(self, s):
        self.line(0, s)

    def mate(self, s):
        self.line(1, s)

    def finish(self):
        net = self.net
        far = lax.rem(net.z + 4, NZ)
        self.up[3, 0].wait_recv()
        self.seen(net.yl, far)
        self.down[3, 1].wait_recv()
        self.seen(1 - net.yl, far)


def kernel(
    slot_ref, a_ref, g_ref, b_ref, o_ref, m1_ref, m2_ref, r_out, s_out, u_out,
    acts, cot, turned, psend, prec, tg, gx0, gy0, gy1, gx1,
    cb, tb, bx0, by0, by1, bx1, tc, cx0, cy0, cy1, cx1, bfull, bturn,
    co, to, ox0, oy0, oy1, ox1, oall,
    m1, m2, mb, cm, tm, mx0, my0, my1, mx1, mfin,
    gall, lfull, stat, smate, dfull, kbuf,
    rall, rpick, rmate, sall, spick, sgot,
    usend, urecv, ylsend, ylrecv, ufin, uall,
    ssem, rsem, asend, arecv, lsem,
):
    net = Net(ssem, rsem)
    x, yh, c, yl, z = net.x, net.yh, net.c, net.yl, net.z
    dp = lax.axis_index("dp")
    home = x * 2 + yh
    oc = 1 - c

    barrier = pltpu.get_barrier_semaphore()
    others = [
        net.at(x=lax.rem(x + i, NX), yh=lax.rem(yh + j, 2), c=lax.rem(c + k, 2))
        for i in range(4) for j in range(2) for k in range(2) if (i, j, k) != (0, 0, 0)
    ]
    others += [net.at(yl=1 - yl), net.at(z=lax.rem(z + 1, NZ)), net.at(z=lax.rem(z + NZ - 1, NZ))]
    for device in others:
        pl.semaphore_signal(barrier, inc=1, device_id=device, device_id_type=MESH)

    def pick(b):
        local = slot_ref[b] - (dp - c) * 2
        inside = (local >= 0) & (local < 4)
        return jnp.where(inside, lax.rem(local + 2 * c + 4, 4), 4)

    def block_of(group, s):
        found = 8
        for b in range(NB):
            found = jnp.where(slot_ref[b] == group * 2 + s, b, found)
        return found

    half_lanes = pl.ds(pl.multiple_of(c * 512, 512), 512)
    other_lanes = pl.ds(pl.multiple_of(oc * 512, 512), 512)
    half_b = pl.ds(pl.multiple_of(c * 1024, 1024), 1024)
    other_b = pl.ds(pl.multiple_of(oc * 1024, 1024), 1024)
    half_o = pl.ds(pl.multiple_of(c * 32, 32), 32)
    other_o = pl.ds(pl.multiple_of(oc * 32, 32), 32)

    def load(i, src, dst):
        copy = pltpu.make_async_copy(src, dst, lsem.at[i])
        copy.start()
        return copy

    load_o = load(0, o_ref.at[:, half_o, :], co.at[pl.ds(0, 2)])
    load_b = load(1, b_ref.at[:, half_b, :], cb.at[pl.ds(0, 2)])
    load_a = load(2, a_ref, acts)
    load_g = load(3, g_ref, cot)
    load_m = [load(4, m1_ref, m1), load(5, m2_ref, m2)]
    cb[4] = jnp.zeros_like(cb[4])
    co[4] = jnp.zeros_like(co[4])
    cm[4] = jnp.zeros_like(cm[4])
    pl.semaphore_wait(barrier, len(others))

    ocopy = net.mate(o_ref.at[:, other_o, :], co.at[pl.ds(2, 2)])
    bcopy = net.mate(b_ref.at[:, other_b, :], cb.at[pl.ds(2, 2)])

    def chooser(chunks, held, first=0):
        def body(b, carry):
            chunks[b // 2, b % 2] = held[pick(b), pl.ds(first, chunks.shape[2]), :]
            return carry

        lax.fori_loop(0, NB, body, 0)

    mine = gall.at[yl, z]

    def statistic(a, b):
        at = pl.multiple_of((a * NZ + b) * 128, 128)
        stat[:, pl.ds(at, 128)] = nt(mine[...], gall[a, b])

    right = Scatter(net, to, (ox0, oy0, oy1, ox1), oall.at[yl, z, c], BF, 16)
    head_b = pl.ds(pl.multiple_of(c * 1024, 128), 384)
    tail_b = pl.ds(pl.multiple_of(c * 1024 + 384, 128), 640)
    left = Scatter(net, tb, (bx0, by0, by1, bx1), bfull.at[head_b], BF, 64)
    rest = Scatter(net, tc, (cx0, cy0, cy1, cx1), bfull.at[tail_b], BF, 64)
    moments = Scatter(net, tm, (mx0, my0, my1, mx1), mfin, BF, 32)
    grads = Scatter(net, tg, (gx0, gy0, gy1, gx1), gall.at[yl, z], F32, 32)
    oring = Ring(net, lambda a, b: oall.at[a, b, c], lambda a, b: None)
    gring = Ring(net, lambda a, b: gall.at[a, b], statistic)

    load_a.wait()
    turned[...] = acts[...].T
    load_o.wait()
    ocopy.wait_recv()
    chooser(to, co)
    right.start()
    load_g.wait()
    of_block = lax.broadcasted_iota(jnp.int32, (128, 2048), 1) % NB

    def product(pair, lanes):
        rows = [
            jnp.where(of_block == 2 * pair + i, turned[...], jnp.zeros((), BF)) for i in range(2)
        ]
        return nn(jnp.concatenate(rows, axis=0), cot[:, lanes]).reshape(2, 128, 512)

    pcopies = []
    for pair in range(4):
        psend[pair] = product(pair, other_lanes).astype(BF)
        pcopies.append(net.mate(psend.at[pair], prec.at[pair]))
    right.middle()
    load_b.wait()
    bcopy.wait_recv()
    chooser(tb, cb)
    left.start()
    for pair in range(4):
        own = product(pair, half_lanes)
        pcopies[pair].wait_recv()
        tg[pair] = (own + prec[pair].astype(F32)).astype(BF)
    grads.start()

    right.finish()
    oring.start()
    for copy in load_m:
        copy.wait()
    for s in range(2):
        mb[s, 0:128, :] = m1[s].astype(BF)
        mb[s, 128:256, :] = m2[s].astype(BF)
    mcopy = net.mate(mb.at[:, :, other_lanes], cm.at[pl.ds(2, 2)])
    for s in range(2):
        cm[s] = mb[s, :, half_lanes]
    chooser(tc, cb, 384)
    oring.own(1)
    mcopy.wait_recv()
    chooser(tm, cm)
    oring.own(2)

    grads.middle()
    left.middle()
    rest.start_x()
    oring.mate(0)
    oring.own(3)
    grads.finish()
    gring.start()
    rest.start_y()
    moments.start()
    oring.mate(1)
    gring.own(1)
    gring.mate(0)
    left.finish()
    gring.own(2)
    oring.mate(2)
    gring.mate(1)
    oring.mate(3)
    rest.middle()
    gring.own(3)
    gring.mate(2)
    oring.finish()
    omate = net.mate(oall.at[:, :, c], oall.at[:, :, c])
    gring.mate(3)
    moments.middle()
    rest.finish()
    bmate = net.mate(bfull.at[half_b], bfull.at[half_b])
    gring.finish()
    bmate.wait_recv()
    bturn[...] = bfull[...].T

    lfull[:, half_lanes] = nn(bturn[...], gall[...].reshape(2048, 512)).astype(BF)
    lmate = net.mate(lfull.at[:, half_lanes], lfull.at[:, half_lanes])
    mine_s = pl.ds(pl.multiple_of(c * 64, 64), 64)
    other_s = pl.ds(pl.multiple_of(oc * 64, 64), 64)
    cstat = net.mate(stat.at[other_s, :], smate)
    cstat.wait_recv()
    sall[x, yh] = (stat[mine_s, :] + smate[...]).astype(BF)
    sspread = Spread(net, sall)
    sspread.start()
    lmate.wait_recv()
    omate.wait_recv()

    basis = oall[:, :, :, :, half_lanes].reshape(1024, 512)
    rotated = nn(lfull[...], basis)
    rall[x, yh] = rotated.astype(BF)
    moments.finish()
    rspread = Spread(net, rall)
    rspread.start()
    first = 0.9 * mfin[0:128, :].astype(F32) + 0.1 * rotated
    second = 0.95 * mfin[128:256, :].astype(F32) + 0.05 * rotated * rotated
    dfull[:, half_lanes] = (first / jnp.sqrt(second)).astype(BF)
    dmate = net.mate(dfull.at[:, half_lanes], dfull.at[:, half_lanes])
    dmate.wait_recv()
    kbuf[...] = nt(dfull[...], oall[c].reshape(512, 1024)).astype(BF)

    def part(zd, yd):
        at = pl.multiple_of((yd * NZ + zd) * 128, 128)
        return nn(bfull[pl.ds(at, 128), :], kbuf[...])

    hops = {}

    def ring_hop(way, s, yd):
        sign = 1 if way == 0 else -1
        value = part(lax.rem(z + sign * (4 - s) + NZ, NZ), yd)
        if (way, s - 1, yd) in hops:
            hops[way, s - 1, yd].wait_recv()
            value = value + urecv[way, s - 1, yd].astype(F32)
        usend[way, s, yd] = value.astype(BF)
        hops[way, s, yd] = net.send(
            usend.at[way, s, yd], urecv.at[way, s, yd], net.at(z=lax.rem(z + sign + NZ, NZ))
        )

    def ring_step(s):
        for yd in (0, 1):
            for way in (0, 1):
                if s > 0 or way == yd:
                    ring_hop(way, s, yd)

    zero_r = jnp.zeros((128, 512), BF)
    zero_s = jnp.zeros((64, 2048), BF)

    def chosen(ref, zero, group, s):
        b = block_of(group, s)
        b0 = jnp.minimum(b, NB - 1)
        return jnp.where(b < NB, ref[b0 // 2, b0 % 2], zero)

    mate_group = dp - c + oc

    ring_step(0)
    sspread.middle()
    ring_step(1)
    rspread.middle()
    ring_step(2)
    ring_step(3)
    rspread.finish()
    for s in range(2):
        rpick[s] = chosen(rall, zero_r, mate_group, s)
    crm = net.mate(rpick, rmate)

    for way in (0, 1):
        for yd in (0, 1):
            hops[way, 3, yd].wait_recv()

    def final(yd):
        return part(z, yd) + urecv[0, 3, yd].astype(F32) + urecv[1, 3, yd].astype(F32)

    ylsend[...] = final(1 - yl).astype(BF)
    cyl = net.send(ylsend, ylrecv, net.at(yl=1 - yl))
    own = final(yl)
    sspread.finish()
    for s in range(2):
        spick[s] = chosen(sall, zero_s, mate_group, s)
    csm = net.mate(spick, sgot)
    cyl.wait_recv()
    ufin[...] = (own + ylrecv[...].astype(F32)).astype(BF)

    def to_columns(j, k):
        tx, ty = 2 * c + j // 2, j % 2
        here = (tx == x) & (ty == yh) & (k == c)
        src = ufin.at[:, pl.ds(j * 128, 128)]

        def copy():
            return pltpu.make_async_remote_copy(
                src_ref=src,
                dst_ref=uall.at[home],
                send_sem=asend.at[j * 2 + k],
                recv_sem=arecv.at[home],
                device_id=net.at(x=tx, yh=ty, c=k),
                device_id_type=MESH,
            )

        return here, copy

    for j in range(4):
        for k in range(2):
            here, copy = to_columns(j, k)

            @pl.when(jnp.logical_not(here))
            def _(copy=copy):
                copy().start()

            @pl.when(here)
            def _(j=j):
                uall[home] = ufin[:, j * 128 : (j + 1) * 128]

    for s in range(2):
        r_out[s, :, half_lanes] = chosen(rall, zero_r, dp, s)
        s_out[s, mine_s, :] = chosen(sall, zero_s, dp, s)
    crm.wait_recv()
    csm.wait_recv()
    for s in range(2):
        r_out[s, :, other_lanes] = rmate[s]
        s_out[s, other_s, :] = sgot[s]

    for b in range(NB):

        @pl.when(jnp.logical_not((b == home) & (c == x // 2)))
        def _(b=b):
            pltpu.make_async_remote_copy(
                src_ref=uall.at[b],
                dst_ref=uall.at[b],
                send_sem=asend.at[0],
                recv_sem=arecv.at[b],
                device_id=net.at(c=oc),
                device_id_type=MESH,
            ).wait_recv()

        value = uall[b]
        u_out[b] = jnp.where(c == 0, value[:, 0:64], value[:, 64:128]).T

    net.drain()
    for j in range(4):
        for k in range(2):
            here, copy = to_columns(j, k)

            @pl.when(jnp.logical_not(here))
            def _(copy=copy):
                copy().wait_send()


def scatter_bufs(rows, lanes):
    h = rows // 2
    return [
        pltpu.VMEM((4, 2, rows, lanes), BF),
        pltpu.VMEM((3, 2, h, lanes), BF),
        pltpu.VMEM((h, lanes), BF),
        pltpu.VMEM((4, h, lanes), BF),
        pltpu.VMEM((3, h, lanes), BF),
    ]


def step(block_slot, acts, cotangent, basis_in, basis_out, moment_first, moment_second):
    vmem = pl.BlockSpec(memory_space=pltpu.VMEM)
    scratch = (
        [
            pltpu.VMEM((2048, 128), BF),
            pltpu.VMEM((2048, 1024), BF),
            pltpu.VMEM((128, 2048), BF),
            pltpu.VMEM((4, 2, 128, 512), BF),
            pltpu.VMEM((4, 2, 128, 512), BF),
        ]
        + scatter_bufs(128, 512)
        + [pltpu.VMEM((5, 1024, 128), BF)] + scatter_bufs(384, 128) + scatter_bufs(640, 128)
        + [pltpu.VMEM((2048, 128), BF), pltpu.VMEM((128, 2048), BF)]
        + [pltpu.VMEM((5, 32, 1024), BF)] + scatter_bufs(32, 1024)
        + [pltpu.VMEM((2, 8, 2, 32, 1024), BF)]
        + [pltpu.VMEM((2, 128, 1024), F32), pltpu.VMEM((2, 128, 1024), F32)]
        + [pltpu.VMEM((2, 256, 1024), BF), pltpu.VMEM((5, 256, 512), BF)] + scatter_bufs(256, 512)
        + [pltpu.VMEM((256, 512), BF)]
        + [
            pltpu.VMEM((2, 8, 128, 512), BF),
            pltpu.VMEM((128, 1024), BF),
            pltpu.VMEM((128, 2048), F32),
            pltpu.VMEM((64, 2048), F32),
            pltpu.VMEM((128, 1024), BF),
            pltpu.VMEM((128, 512), BF),
            pltpu.VMEM((4, 2, 128, 512), BF),
            pltpu.VMEM((2, 128, 512), BF),
            pltpu.VMEM((2, 128, 512), BF),
            pltpu.VMEM((4, 2, 64, 2048), BF),
            pltpu.VMEM((2, 64, 2048), BF),
            pltpu.VMEM((2, 64, 2048), BF),
            pltpu.VMEM((2, 4, 2, 128, 512), BF),
            pltpu.VMEM((2, 4, 2, 128, 512), BF),
            pltpu.VMEM((128, 512), BF),
            pltpu.VMEM((128, 512), BF),
            pltpu.VMEM((128, 512), BF),
            pltpu.VMEM((8, 128, 128), BF),
            pltpu.SemaphoreType.DMA((128,)),
            pltpu.SemaphoreType.DMA((128,)),
            pltpu.SemaphoreType.DMA((8,)),
            pltpu.SemaphoreType.DMA((8,)),
            pltpu.SemaphoreType.DMA((6,)),
        ]
    )
    return pl.pallas_call(
        kernel,
        out_shape=(
            jax.ShapeDtypeStruct((2, 128, 1024), BF),
            jax.ShapeDtypeStruct((2, 128, 2048), BF),
            jax.ShapeDtypeStruct((8, 64, 128), BF),
        ),
        in_specs=[pl.BlockSpec(memory_space=pltpu.SMEM)] + [pl.BlockSpec(memory_space=pl.ANY)] * 6,
        out_specs=(vmem, vmem, vmem),
        scratch_shapes=scratch,
        compiler_params=pltpu.CompilerParams(
            collective_id=0, has_side_effects=True, vmem_limit_bytes=56 << 20
        ),
        name="soap_step",
    )(block_slot, acts, cotangent, basis_in, basis_out, moment_first, moment_second)


def per_device(acts, cotangent, block_slot, basis_in, basis_out, moment_first, moment_second):
    rotated, stat, update = step(
        block_slot,
        acts.reshape(-1, acts.shape[2]),
        cotangent.reshape(-1, cotangent.shape[2]),
        basis_in,
        basis_out,
        moment_first,
        moment_second,
    )
    rotated = rotated.astype(F32)
    new_first = 0.9 * moment_first + 0.1 * rotated
    new_second = 0.95 * moment_second + 0.05 * rotated * rotated
    return (new_first, new_second, stat.astype(F32), jnp.swapaxes(update, 1, 2))


def solution(mesh):
    placed = (
        P("dp", None, "mp"),
        P("dp", None, None),
        P(),
        P("dp", None, "mp"),
        P("dp", "mp", None),
        P("dp", "mp", None),
        P("dp", "mp", None),
    )
    return jax.shard_map(
        per_device,
        mesh=mesh,
        in_specs=placed,
        out_specs=(
            P("dp", "mp", None),
            P("dp", "mp", None),
            P("dp", "mp", None),
            P(None, "mp", "dp"),
        ),
        check_vma=False,
    )
```

```python
import functools

import jax
import jax.numpy as jnp
from jax import lax
from jax.experimental import pallas as pl
from jax.experimental.pallas import tpu as pltpu
from jax.sharding import PartitionSpec as P

MESH = pl.DeviceIdType.MESH
BF = jnp.bfloat16
F32 = jnp.float32
NX, NZ = 4, 8
NB = 8


def nt(a, b):
    return lax.dot_general(a, b, (((1,), (1,)), ((), ())), preferred_element_type=F32)


def nn(a, b):
    return jnp.dot(a, b, preferred_element_type=F32)


def tn(a, b):
    return lax.dot_general(a, b, (((0,), (0,)), ((), ())), preferred_element_type=F32)


class Net:
    def __init__(self, ssem, rsem):
        self.ssem, self.rsem, self.used, self.sent = ssem, rsem, 0, []
        dp, mp = lax.axis_index("dp"), lax.axis_index("mp")
        self.x, self.yh, self.c = dp // 4, (dp // 2) % 2, dp % 2
        self.yl, self.z = mp // NZ, mp % NZ

    def at(self, x=None, yh=None, c=None, yl=None, z=None):
        x = self.x if x is None else x
        yh = self.yh if yh is None else yh
        c = self.c if c is None else c
        yl = self.yl if yl is None else yl
        z = self.z if z is None else z
        return (x * 4 + yh * 2 + c, yl * NZ + z)

    def send(self, src, dst, device):
        i = self.used
        self.used += 1
        copy = pltpu.make_async_remote_copy(
            src_ref=src,
            dst_ref=dst,
            send_sem=self.ssem.at[i],
            recv_sem=self.rsem.at[i],
            device_id=device,
            device_id_type=MESH,
        )
        copy.start()
        self.sent.append(copy)
        return copy

    def drain(self):
        for copy in self.sent:
            copy.wait_send()

    def mate(self, src, dst):
        return self.send(src, dst, self.at(c=1 - self.c))

    def xs(self):
        return [lax.rem(self.x + k, NX) for k in (1, 2, 3)]


class Scatter:
    def __init__(self, net, t, bufs, out, kind, step):
        self.net, self.t, self.out, self.kind, self.step = net, t, out, kind, step
        self.x0, self.y0, self.y1, self.x1 = bufs
        self.half = self.y0.shape[0]
        self.left = t.shape[2] - self.half

    def start_x(self):
        net, h = self.net, self.half
        self.cx0 = [
            net.send(self.t.at[xp, :, pl.ds(0, h), :], self.x0.at[k], net.at(x=xp))
            for k, xp in enumerate(net.xs())
        ]

    def start_y(self):
        net, h = self.net, self.half
        self.cy1 = net.send(
            self.t.at[:, 1 - net.yh, pl.ds(h, self.left), :], self.y1, net.at(yh=1 - net.yh)
        )

    def start(self):
        self.start_y()
        self.start_x()

    def add(self, dst, srcs, count):
        n, kind = self.step, self.kind

        def body(i, carry):
            rows = pl.ds(pl.multiple_of(i * n, n), n)
            total = None
            for src in srcs:
                part = src(rows).astype(kind)
                total = part if total is None else total + part
            dst(rows, total.astype(BF))
            return carry

        lax.fori_loop(0, count // n, body, 0)

    def rows_of(self, ref, base=0):
        def load(rows):
            return ref[pl.ds(pl.multiple_of(rows.start + base, 16), rows.size), :]

        return load

    def store_of(self, ref, base=0):
        def store(rows, value):
            ref[pl.ds(pl.multiple_of(rows.start + base, 16), rows.size), :] = value

        return store

    def middle(self):
        net, h, t = self.net, self.half, self.t
        for copy in self.cx0:
            copy.wait_recv()
        for yp in (1 - net.yh, net.yh):
            mine = t.at[net.x, yp]
            self.add(
                self.store_of(mine),
                [self.rows_of(mine)] + [self.rows_of(self.x0.at[k, yp]) for k in range(3)],
                h,
            )
            if yp is not net.yh:
                self.cy0 = net.send(
                    t.at[net.x, 1 - net.yh, pl.ds(0, h), :], self.y0, net.at(yh=1 - net.yh)
                )
        self.cy1.wait_recv()
        self.cx1 = []
        for k, xp in enumerate(net.xs() + [net.x]):
            mine = t.at[xp, net.yh]
            self.add(
                self.store_of(mine, h),
                [self.rows_of(mine, h), self.rows_of(self.y1.at[xp])],
                self.left,
            )
            if k < 3:
                self.cx1.append(
                    net.send(t.at[xp, net.yh, pl.ds(h, self.left), :], self.x1.at[k], net.at(x=xp))
                )

    def finish(self):
        net, h = self.net, self.half
        mine = self.t.at[net.x, net.yh]
        self.cy0.wait_recv()
        self.add(self.store_of(self.out), [self.rows_of(mine), self.rows_of(self.y0)], h)
        for copy in self.cx1:
            copy.wait_recv()
        self.add(
            self.store_of(self.out, h),
            [self.rows_of(mine, h)] + [self.rows_of(self.x1.at[k]) for k in range(3)],
            self.left,
        )


class Spread:
    def __init__(self, net, a):
        self.net, self.a, self.half = net, a, a.shape[2] // 2

    def start(self):
        net, h, a = self.net, self.half, self.a
        last = a.at[net.x, net.yh, pl.ds(h, h), :]
        self.cy = net.send(last, last, net.at(yh=1 - net.yh))
        first = a.at[net.x, net.yh, pl.ds(0, h), :]
        self.cx = [net.send(first, first, net.at(x=xp)) for xp in net.xs()]

    def middle(self):
        net, h, a = self.net, self.half, self.a
        self.cy.wait_recv()
        last = a.at[net.x, :, pl.ds(h, h), :]
        self.cx2 = [net.send(last, last, net.at(x=xp)) for xp in net.xs()]
        for copy in self.cx:
            copy.wait_recv()
        first = a.at[:, net.yh, pl.ds(0, h), :]
        self.cy2 = net.send(first, first, net.at(yh=1 - net.yh))

    def finish(self):
        for copy in self.cx2:
            copy.wait_recv()
        self.cy2.wait_recv()


class Ring:
    def __init__(self, net, block, parts, seen):
        self.net, self.block, self.parts, self.seen = net, block, range(parts), seen
        self.up, self.down = {}, {}

    def hop(self, way, step, line, p):
        net = self.net
        yl = net.yl if line == 0 else 1 - net.yl
        sign = 1 if way == 0 else -1
        ref = self.block(yl, lax.rem(net.z - sign * step + NZ, NZ), p)
        copy = net.send(ref, ref, net.at(z=lax.rem(net.z + sign + NZ, NZ)))
        (self.up if way == 0 else self.down)[step, line, p] = copy

    def start(self):
        net = self.net
        self.cy = []
        for p in self.parts:
            own = self.block(net.yl, net.z, p)
            self.hop(0, 0, 0, p)
            self.hop(1, 0, 0, p)
            self.cy.append(net.send(own, own, net.at(yl=1 - net.yl)))
        self.seen(net.yl, net.z)

    def line(self, line, s):
        net = self.net
        yl = net.yl if line == 0 else 1 - net.yl
        for p in self.parts:
            if s == 0:
                self.cy[p].wait_recv()
                self.hop(0, 0, 1, p)
                self.hop(1, 0, 1, p)
                continue
            self.up[s - 1, line, p].wait_recv()
            if s < 3 or line == 0:
                self.hop(0, s, line, p)
            self.down[s - 1, line, p].wait_recv()
            if s < 3 or line == 1:
                self.hop(1, s, line, p)
        if s == 0:
            self.seen(yl, net.z)
        else:
            self.seen(yl, lax.rem(net.z - s + NZ, NZ))
            self.seen(yl, lax.rem(net.z + s, NZ))

    def own(self, s):
        self.line(0, s)

    def mate(self, s):
        self.line(1, s)

    def finish(self):
        net = self.net
        far = lax.rem(net.z + 4, NZ)
        for p in self.parts:
            self.up[3, 0, p].wait_recv()
        self.seen(net.yl, far)
        for p in self.parts:
            self.down[3, 1, p].wait_recv()
        self.seen(1 - net.yl, far)


def kernel(
    slot_ref, a_ref, g_ref, b_ref, o_ref, m1_ref, m2_ref, r_out, s_out, u_out,
    acts, cot, turned, psend, prec, tg, gx0, gy0, gy1, gx1,
    cb, tb, bx0, by0, by1, bx1, tc, cx0, cy0, cy1, cx1, bfull, bturn,
    co, to, ox0, oy0, oy1, ox1, oall,
    m1, m2, mb, cm, tm, mx0, my0, my1, mx1, mfin,
    gall, lfull, stat, smate, dfull, kbuf,
    rall, rpick, rmate, sall, spick, sgot,
    usend, urecv, ylsend, ylrecv, ufin, uall,
    ssem, rsem, asend, arecv, lsem,
):
    net = Net(ssem, rsem)
    x, yh, c, yl, z = net.x, net.yh, net.c, net.yl, net.z
    dp = lax.axis_index("dp")
    home = x * 2 + yh
    oc = 1 - c

    barrier = pltpu.get_barrier_semaphore()
    others = [
        net.at(x=lax.rem(x + i, NX), yh=lax.rem(yh + j, 2), c=lax.rem(c + k, 2))
        for i in range(4) for j in range(2) for k in range(2) if (i, j, k) != (0, 0, 0)
    ]
    others += [net.at(yl=1 - yl), net.at(z=lax.rem(z + 1, NZ)), net.at(z=lax.rem(z + NZ - 1, NZ))]
    for device in others:
        pl.semaphore_signal(barrier, inc=1, device_id=device, device_id_type=MESH)

    def pick(b):
        local = slot_ref[b] - (dp - c) * 2
        inside = (local >= 0) & (local < 4)
        return jnp.where(inside, lax.rem(local + 2 * c + 4, 4), 4)

    def block_of(group, s):
        found = 8
        for b in range(NB):
            found = jnp.where(slot_ref[b] == group * 2 + s, b, found)
        return found

    half_lanes = pl.ds(pl.multiple_of(c * 512, 512), 512)
    other_lanes = pl.ds(pl.multiple_of(oc * 512, 512), 512)
    half_b = pl.ds(pl.multiple_of(c * 1024, 1024), 1024)
    other_b = pl.ds(pl.multiple_of(oc * 1024, 1024), 1024)
    half_o = pl.ds(pl.multiple_of(c * 32, 32), 32)
    other_o = pl.ds(pl.multiple_of(oc * 32, 32), 32)

    def load(i, src, dst):
        copy = pltpu.make_async_copy(src, dst, lsem.at[i])
        copy.start()
        return copy

    load_o = load(0, o_ref.at[:, half_o, :], co.at[pl.ds(0, 2)])
    load_b = load(1, b_ref.at[:, half_b, :], cb.at[pl.ds(0, 2)])
    load_a = load(2, a_ref, acts)
    load_g = load(3, g_ref, cot)
    load_m = [load(4, m1_ref, m1), load(5, m2_ref, m2)]
    cb[4] = jnp.zeros_like(cb[4])
    co[4] = jnp.zeros_like(co[4])
    cm[4] = jnp.zeros_like(cm[4])
    pl.semaphore_wait(barrier, len(others))

    ocopy = net.mate(o_ref.at[:, other_o, :], co.at[pl.ds(2, 2)])
    bcopy = net.mate(b_ref.at[:, other_b, :], cb.at[pl.ds(2, 2)])

    def chooser(chunks, held, first=0):
        def body(b, carry):
            chunks[b // 2, b % 2] = held[pick(b), pl.ds(first, chunks.shape[2]), :]
            return carry

        lax.fori_loop(0, NB, body, 0)

    mine = gall.at[yl, z]

    def statistic(a, b):
        at = pl.multiple_of((a * NZ + b) * 128, 128)
        stat[:, pl.ds(at, 128)] = nt(mine[...], gall[a, b])

    right = Scatter(net, to, (ox0, oy0, oy1, ox1), oall.at[yl, z, c], BF, 16)
    head_b = pl.ds(pl.multiple_of(c * 1024, 128), 384)
    tail_b = pl.ds(pl.multiple_of(c * 1024 + 384, 128), 640)
    left = Scatter(net, tb, (bx0, by0, by1, bx1), bfull.at[head_b], BF, 64)
    rest = Scatter(net, tc, (cx0, cy0, cy1, cx1), bfull.at[tail_b], BF, 64)
    moments = Scatter(net, tm, (mx0, my0, my1, mx1), mfin, BF, 32)
    grads = Scatter(net, tg, (gx0, gy0, gy1, gx1), gall.at[yl, z], F32, 32)
    oring = Ring(net, lambda a, b, p: oall.at[a, b, c], 1, lambda a, b: None)
    gring = Ring(net, lambda a, b, p: gall.at[a, b, pl.ds(p * 64, 64), :], 2, statistic)

    load_a.wait()
    turned[...] = acts[...].T
    load_o.wait()
    ocopy.wait_recv()
    chooser(to, co)
    right.start()
    load_b.wait()
    bcopy.wait_recv()
    chooser(tb, cb)
    left.start()
    load_g.wait()
    of_block = lax.broadcasted_iota(jnp.int32, (128, 2048), 1) % NB

    def product(pair, lanes):
        rows = [
            jnp.where(of_block == 2 * pair + i, turned[...], jnp.zeros((), BF)) for i in range(2)
        ]
        return nn(jnp.concatenate(rows, axis=0), cot[:, lanes]).reshape(2, 128, 512)

    pcopies = []
    for pair in range(4):
        psend[pair] = product(pair, other_lanes).astype(BF)
        pcopies.append(net.mate(psend.at[pair], prec.at[pair]))
    for pair in range(4):
        own = product(pair, half_lanes)
        pcopies[pair].wait_recv()
        tg[pair] = (own + prec[pair].astype(F32)).astype(BF)
        if pair == 1:
            right.middle()
    grads.start()

    right.finish()
    oring.start()
    for copy in load_m:
        copy.wait()
    for s in range(2):
        mb[s, 0:128, :] = m1[s].astype(BF)
        mb[s, 128:256, :] = m2[s].astype(BF)
    mcopy = net.mate(mb.at[:, :, other_lanes], cm.at[pl.ds(2, 2)])
    for s in range(2):
        cm[s] = mb[s, :, half_lanes]
    chooser(tc, cb, 384)
    oring.own(1)
    mcopy.wait_recv()
    chooser(tm, cm)
    oring.own(2)

    grads.middle()
    left.middle()
    rest.start_x()
    oring.mate(0)
    oring.own(3)
    grads.finish()
    gring.start()
    moments.start_x()
    oring.mate(1)
    gring.own(1)
    gring.mate(0)
    rest.start_y()
    moments.start_y()
    left.finish()
    gring.own(2)
    oring.mate(2)
    gring.mate(1)
    oring.mate(3)
    gring.own(3)
    rest.middle()
    gring.mate(2)
    oring.finish()
    omate = net.mate(oall.at[:, :, c], oall.at[:, :, c])
    gring.mate(3)
    moments.middle()
    rest.finish()
    bmate = net.mate(bfull.at[half_b], bfull.at[half_b])
    gring.finish()
    bmate.wait_recv()
    bturn[...] = bfull[...].T

    lfull[:, half_lanes] = nn(bturn[...], gall[...].reshape(2048, 512)).astype(BF)
    lmate = net.mate(lfull.at[:, half_lanes], lfull.at[:, half_lanes])
    mine_s = pl.ds(pl.multiple_of(c * 64, 64), 64)
    other_s = pl.ds(pl.multiple_of(oc * 64, 64), 64)
    cstat = net.mate(stat.at[other_s, :], smate)
    cstat.wait_recv()
    sall[x, yh] = (stat[mine_s, :] + smate[...]).astype(BF)
    sspread = Spread(net, sall)
    sspread.start()
    lmate.wait_recv()
    omate.wait_recv()

    basis = oall[:, :, :, :, half_lanes].reshape(1024, 512)
    rotated = nn(lfull[...], basis)
    rall[x, yh] = rotated.astype(BF)
    moments.finish()
    rspread = Spread(net, rall)
    rspread.start()
    first = 0.9 * mfin[0:128, :].astype(F32) + 0.1 * rotated
    second = 0.95 * mfin[128:256, :].astype(F32) + 0.05 * rotated * rotated
    dfull[:, half_lanes] = (first / jnp.sqrt(second)).astype(BF)
    dmate = net.mate(dfull.at[:, half_lanes], dfull.at[:, half_lanes])
    dmate.wait_recv()
    kbuf[...] = nt(dfull[...], oall[c].reshape(512, 1024)).astype(BF)

    def part(zd, yd, p):
        at = pl.multiple_of((yd * NZ + zd) * 128 + p * 64, 64)
        return nn(bfull[pl.ds(at, 64), :], kbuf[...])

    hops = {}
    lines = (1 - yl, yl)

    def ring_hop(way, line, s):
        sign = 1 if way == 0 else -1
        for p in range(2):
            value = part(lax.rem(z + sign * (4 - s) + NZ, NZ), lines[line], p)
            if (way, line, s - 1, p) in hops:
                hops[way, line, s - 1, p].wait_recv()
                value = value + urecv[way, s - 1, line, p].astype(F32)
            usend[way, s, line, p] = value.astype(BF)
            hops[way, line, s, p] = net.send(
                usend.at[way, s, line, p],
                urecv.at[way, s, line, p],
                net.at(z=lax.rem(z + sign + NZ, NZ)),
            )

    zero_r = jnp.zeros((128, 512), BF)
    zero_s = jnp.zeros((64, 2048), BF)

    def chosen(ref, zero, group, s):
        b = block_of(group, s)
        b0 = jnp.minimum(b, NB - 1)
        return jnp.where(b < NB, ref[b0 // 2, b0 % 2], zero)

    mate_group = dp - c + oc

    ring_hop(0, 0, 0)
    ring_hop(1, 1, 0)
    ring_hop(0, 1, 1)
    ring_hop(1, 0, 1)
    sspread.middle()
    ring_hop(0, 0, 1)
    ring_hop(1, 1, 1)
    ring_hop(0, 1, 2)
    ring_hop(1, 0, 2)
    rspread.middle()
    ring_hop(0, 0, 2)
    ring_hop(1, 1, 2)
    ring_hop(1, 0, 3)
    ring_hop(0, 0, 3)
    ring_hop(0, 1, 3)
    ring_hop(1, 1, 3)
    rspread.finish()
    for s in range(2):
        rpick[s] = chosen(rall, zero_r, mate_group, s)
    crm = net.mate(rpick, rmate)

    def final(line, p):
        for way in (0, 1):
            hops[way, line, 3, p].wait_recv()
        here = part(z, lines[line], p)
        return here + urecv[0, 3, line, p].astype(F32) + urecv[1, 3, line, p].astype(F32)

    cyl = []
    for p in range(2):
        ylsend[p] = final(0, p).astype(BF)
        cyl.append(net.send(ylsend.at[p], ylrecv.at[p], net.at(yl=1 - yl)))
    sspread.finish()
    for s in range(2):
        spick[s] = chosen(sall, zero_s, mate_group, s)
    csm = net.mate(spick, sgot)
    for p in range(2):
        own = final(1, p)
        cyl[p].wait_recv()
        ufin[p * 64 : (p + 1) * 64, :] = (own + ylrecv[p].astype(F32)).astype(BF)

    def to_columns(j, k):
        tx, ty = 2 * c + j // 2, j % 2
        here = (tx == x) & (ty == yh) & (k == c)
        src = ufin.at[:, pl.ds(j * 128, 128)]

        def copy():
            return pltpu.make_async_remote_copy(
                src_ref=src,
                dst_ref=uall.at[home],
                send_sem=asend.at[j * 2 + k],
                recv_sem=arecv.at[home],
                device_id=net.at(x=tx, yh=ty, c=k),
                device_id_type=MESH,
            )

        return here, copy

    for j in range(4):
        for k in range(2):
            here, copy = to_columns(j, k)

            @pl.when(jnp.logical_not(here))
            def _(copy=copy):
                copy().start()

            @pl.when(here)
            def _(j=j):
                uall[home] = ufin[:, j * 128 : (j + 1) * 128]

    for s in range(2):
        r_out[s, :, half_lanes] = chosen(rall, zero_r, dp, s)
        s_out[s, mine_s, :] = chosen(sall, zero_s, dp, s)
    crm.wait_recv()
    csm.wait_recv()
    for s in range(2):
        r_out[s, :, other_lanes] = rmate[s]
        s_out[s, other_s, :] = sgot[s]

    for b in range(NB):

        @pl.when(jnp.logical_not((b == home) & (c == x // 2)))
        def _(b=b):
            pltpu.make_async_remote_copy(
                src_ref=uall.at[b],
                dst_ref=uall.at[b],
                send_sem=asend.at[0],
                recv_sem=arecv.at[b],
                device_id=net.at(c=oc),
                device_id_type=MESH,
            ).wait_recv()

        value = uall[b]
        u_out[b] = jnp.where(c == 0, value[:, 0:64], value[:, 64:128]).T

    net.drain()
    for j in range(4):
        for k in range(2):
            here, copy = to_columns(j, k)

            @pl.when(jnp.logical_not(here))
            def _(copy=copy):
                copy().wait_send()


def scatter_bufs(rows, lanes, h=None):
    h = rows // 2 if h is None else h
    return [
        pltpu.VMEM((4, 2, rows, lanes), BF),
        pltpu.VMEM((3, 2, h, lanes), BF),
        pltpu.VMEM((h, lanes), BF),
        pltpu.VMEM((4, rows - h, lanes), BF),
        pltpu.VMEM((3, rows - h, lanes), BF),
    ]


def step(block_slot, acts, cotangent, basis_in, basis_out, moment_first, moment_second):
    vmem = pl.BlockSpec(memory_space=pltpu.VMEM)
    scratch = (
        [
            pltpu.VMEM((2048, 128), BF),
            pltpu.VMEM((2048, 1024), BF),
            pltpu.VMEM((128, 2048), BF),
            pltpu.VMEM((4, 2, 128, 512), BF),
            pltpu.VMEM((4, 2, 128, 512), BF),
        ]
        + scatter_bufs(128, 512)
        + [pltpu.VMEM((5, 1024, 128), BF)] + scatter_bufs(384, 128) + scatter_bufs(640, 128)
        + [pltpu.VMEM((2048, 128), BF), pltpu.VMEM((128, 2048), BF)]
        + [pltpu.VMEM((5, 32, 1024), BF)] + scatter_bufs(32, 1024)
        + [pltpu.VMEM((2, 8, 2, 32, 1024), BF)]
        + [pltpu.VMEM((2, 128, 1024), F32), pltpu.VMEM((2, 128, 1024), F32)]
        + [pltpu.VMEM((2, 256, 1024), BF), pltpu.VMEM((5, 256, 512), BF)] + scatter_bufs(256, 512, 160)
        + [pltpu.VMEM((256, 512), BF)]
        + [
            pltpu.VMEM((2, 8, 128, 512), BF),
            pltpu.VMEM((128, 1024), BF),
            pltpu.VMEM((128, 2048), F32),
            pltpu.VMEM((64, 2048), F32),
            pltpu.VMEM((128, 1024), BF),
            pltpu.VMEM((128, 512), BF),
            pltpu.VMEM((4, 2, 128, 512), BF),
            pltpu.VMEM((2, 128, 512), BF),
            pltpu.VMEM((2, 128, 512), BF),
            pltpu.VMEM((4, 2, 64, 2048), BF),
            pltpu.VMEM((2, 64, 2048), BF),
            pltpu.VMEM((2, 64, 2048), BF),
            pltpu.VMEM((2, 4, 2, 2, 64, 512), BF),
            pltpu.VMEM((2, 4, 2, 2, 64, 512), BF),
            pltpu.VMEM((2, 64, 512), BF),
            pltpu.VMEM((2, 64, 512), BF),
            pltpu.VMEM((128, 512), BF),
            pltpu.VMEM((8, 128, 128), BF),
            pltpu.SemaphoreType.DMA((192,)),
            pltpu.SemaphoreType.DMA((192,)),
            pltpu.SemaphoreType.DMA((8,)),
            pltpu.SemaphoreType.DMA((8,)),
            pltpu.SemaphoreType.DMA((6,)),
        ]
    )
    return pl.pallas_call(
        kernel,
        out_shape=(
            jax.ShapeDtypeStruct((2, 128, 1024), BF),
            jax.ShapeDtypeStruct((2, 128, 2048), BF),
            jax.ShapeDtypeStruct((8, 64, 128), BF),
        ),
        in_specs=[pl.BlockSpec(memory_space=pltpu.SMEM)] + [pl.BlockSpec(memory_space=pl.ANY)] * 6,
        out_specs=(vmem, vmem, vmem),
        scratch_shapes=scratch,
        compiler_params=pltpu.CompilerParams(
            collective_id=0, has_side_effects=True, vmem_limit_bytes=56 << 20
        ),
        name="soap_step",
    )(block_slot, acts, cotangent, basis_in, basis_out, moment_first, moment_second)


def per_device(acts, cotangent, block_slot, basis_in, basis_out, moment_first, moment_second):
    rotated, stat, update = step(
        block_slot,
        acts.reshape(-1, acts.shape[2]),
        cotangent.reshape(-1, cotangent.shape[2]),
        basis_in,
        basis_out,
        moment_first,
        moment_second,
    )
    rotated = rotated.astype(F32)
    new_first = 0.9 * moment_first + 0.1 * rotated
    new_second = 0.95 * moment_second + 0.05 * rotated * rotated
    return (new_first, new_second, stat.astype(F32), jnp.swapaxes(update, 1, 2))


def solution(mesh):
    placed = (
        P("dp", None, "mp"),
        P("dp", None, None),
        P(),
        P("dp", None, "mp"),
        P("dp", "mp", None),
        P("dp", "mp", None),
        P("dp", "mp", None),
    )
    return jax.shard_map(
        per_device,
        mesh=mesh,
        in_specs=placed,
        out_specs=(
            P("dp", "mp", None),
            P("dp", "mp", None),
            P("dp", "mp", None),
            P(None, "mp", "dp"),
        ),
        check_vma=False,
    )
```

```python
import functools

import jax
import jax.numpy as jnp
from jax import lax
from jax.experimental import pallas as pl
from jax.experimental.pallas import tpu as pltpu
from jax.sharding import PartitionSpec as P

MESH = pl.DeviceIdType.MESH
BF = jnp.bfloat16
F32 = jnp.float32
NX, NZ = 4, 8
NB = 8


def nt(a, b):
    return lax.dot_general(a, b, (((1,), (1,)), ((), ())), preferred_element_type=F32)


def nn(a, b):
    return jnp.dot(a, b, preferred_element_type=F32)


def tn(a, b):
    return lax.dot_general(a, b, (((0,), (0,)), ((), ())), preferred_element_type=F32)


class Net:
    def __init__(self, ssem, rsem):
        self.ssem, self.rsem, self.used, self.sent = ssem, rsem, 0, []
        dp, mp = lax.axis_index("dp"), lax.axis_index("mp")
        self.x, self.yh, self.c = dp // 4, (dp // 2) % 2, dp % 2
        self.yl, self.z = mp // NZ, mp % NZ

    def at(self, x=None, yh=None, c=None, yl=None, z=None):
        x = self.x if x is None else x
        yh = self.yh if yh is None else yh
        c = self.c if c is None else c
        yl = self.yl if yl is None else yl
        z = self.z if z is None else z
        return (x * 4 + yh * 2 + c, yl * NZ + z)

    def send(self, src, dst, device):
        i = self.used
        self.used += 1
        copy = pltpu.make_async_remote_copy(
            src_ref=src,
            dst_ref=dst,
            send_sem=self.ssem.at[i],
            recv_sem=self.rsem.at[i],
            device_id=device,
            device_id_type=MESH,
        )
        copy.start()
        self.sent.append(copy)
        return copy

    def drain(self):
        for copy in self.sent:
            copy.wait_send()

    def mate(self, src, dst):
        return self.send(src, dst, self.at(c=1 - self.c))

    def xs(self):
        return [lax.rem(self.x + k, NX) for k in (1, 2, 3)]


class Scatter:
    def __init__(self, net, t, bufs, out, kind, step):
        self.net, self.t, self.out, self.kind, self.step = net, t, out, kind, step
        self.x0, self.y0, self.y1, self.x1 = bufs
        self.half = self.y0.shape[0]
        self.left = t.shape[2] - self.half

    def start_x(self):
        net, h = self.net, self.half
        self.cx0 = [
            net.send(self.t.at[xp, :, pl.ds(0, h), :], self.x0.at[k], net.at(x=xp))
            for k, xp in enumerate(net.xs())
        ]

    def start_y(self):
        net, h = self.net, self.half
        self.cy1 = net.send(
            self.t.at[:, 1 - net.yh, pl.ds(h, self.left), :], self.y1, net.at(yh=1 - net.yh)
        )

    def start(self):
        self.start_y()
        self.start_x()

    def add(self, dst, srcs, count):
        n, kind = self.step, self.kind

        def body(i, carry):
            rows = pl.ds(pl.multiple_of(i * n, n), n)
            total = None
            for src in srcs:
                part = src(rows).astype(kind)
                total = part if total is None else total + part
            dst(rows, total.astype(BF))
            return carry

        lax.fori_loop(0, count // n, body, 0)

    def rows_of(self, ref, base=0):
        def load(rows):
            return ref[pl.ds(pl.multiple_of(rows.start + base, 16), rows.size), :]

        return load

    def store_of(self, ref, base=0):
        def store(rows, value):
            ref[pl.ds(pl.multiple_of(rows.start + base, 16), rows.size), :] = value

        return store

    def middle(self):
        net, h, t = self.net, self.half, self.t
        for copy in self.cx0:
            copy.wait_recv()
        for yp in (1 - net.yh, net.yh):
            mine = t.at[net.x, yp]
            self.add(
                self.store_of(mine),
                [self.rows_of(mine)] + [self.rows_of(self.x0.at[k, yp]) for k in range(3)],
                h,
            )
            if yp is not net.yh:
                self.cy0 = net.send(
                    t.at[net.x, 1 - net.yh, pl.ds(0, h), :], self.y0, net.at(yh=1 - net.yh)
                )
        self.cy1.wait_recv()
        self.cx1 = []
        for k, xp in enumerate(net.xs() + [net.x]):
            mine = t.at[xp, net.yh]
            self.add(
                self.store_of(mine, h),
                [self.rows_of(mine, h), self.rows_of(self.y1.at[xp])],
                self.left,
            )
            if k < 3:
                self.cx1.append(
                    net.send(t.at[xp, net.yh, pl.ds(h, self.left), :], self.x1.at[k], net.at(x=xp))
                )

    def finish(self):
        net, h = self.net, self.half
        mine = self.t.at[net.x, net.yh]
        self.cy0.wait_recv()
        self.add(self.store_of(self.out), [self.rows_of(mine), self.rows_of(self.y0)], h)
        for copy in self.cx1:
            copy.wait_recv()
        self.add(
            self.store_of(self.out, h),
            [self.rows_of(mine, h)] + [self.rows_of(self.x1.at[k]) for k in range(3)],
            self.left,
        )


class Spread:
    def __init__(self, net, a):
        self.net, self.a, self.half = net, a, a.shape[2] // 2

    def start(self):
        net, h, a = self.net, self.half, self.a
        last = a.at[net.x, net.yh, pl.ds(h, h), :]
        self.cy = net.send(last, last, net.at(yh=1 - net.yh))
        first = a.at[net.x, net.yh, pl.ds(0, h), :]
        self.cx = [net.send(first, first, net.at(x=xp)) for xp in net.xs()]

    def middle(self):
        net, h, a = self.net, self.half, self.a
        self.cy.wait_recv()
        last = a.at[net.x, :, pl.ds(h, h), :]
        self.cx2 = [net.send(last, last, net.at(x=xp)) for xp in net.xs()]
        for copy in self.cx:
            copy.wait_recv()
        first = a.at[:, net.yh, pl.ds(0, h), :]
        self.cy2 = net.send(first, first, net.at(yh=1 - net.yh))

    def finish(self):
        for copy in self.cx2:
            copy.wait_recv()
        self.cy2.wait_recv()


class Ring:
    def __init__(self, net, block, parts, seen):
        self.net, self.block, self.parts, self.seen = net, block, range(parts), seen
        self.up, self.down = {}, {}

    def hop(self, way, step, line, p):
        net = self.net
        yl = net.yl if line == 0 else 1 - net.yl
        sign = 1 if way == 0 else -1
        ref = self.block(yl, lax.rem(net.z - sign * step + NZ, NZ), p)
        copy = net.send(ref, ref, net.at(z=lax.rem(net.z + sign + NZ, NZ)))
        (self.up if way == 0 else self.down)[step, line, p] = copy

    def start(self):
        net = self.net
        self.cy = []
        for p in self.parts:
            own = self.block(net.yl, net.z, p)
            self.hop(0, 0, 0, p)
            self.hop(1, 0, 0, p)
            self.cy.append(net.send(own, own, net.at(yl=1 - net.yl)))
        self.seen(net.yl, net.z)

    def line(self, line, s):
        net = self.net
        yl = net.yl if line == 0 else 1 - net.yl
        for p in self.parts:
            if s == 0:
                self.cy[p].wait_recv()
                self.hop(0, 0, 1, p)
                self.hop(1, 0, 1, p)
                continue
            self.up[s - 1, line, p].wait_recv()
            if s < 3 or line == 0:
                self.hop(0, s, line, p)
            self.down[s - 1, line, p].wait_recv()
            if s < 3 or line == 1:
                self.hop(1, s, line, p)
        if s == 0:
            self.seen(yl, net.z)
        else:
            self.seen(yl, lax.rem(net.z - s + NZ, NZ))
            self.seen(yl, lax.rem(net.z + s, NZ))

    def own(self, s):
        self.line(0, s)

    def mate(self, s):
        self.line(1, s)

    def finish(self):
        net = self.net
        far = lax.rem(net.z + 4, NZ)
        for p in self.parts:
            self.up[3, 0, p].wait_recv()
        self.seen(net.yl, far)
        for p in self.parts:
            self.down[3, 1, p].wait_recv()
        self.seen(1 - net.yl, far)


def kernel(
    slot_ref, a_ref, g_ref, b_ref, o_ref, m1_ref, m2_ref, r_out, s_out, u_out,
    acts, cot, turned, psend, prec, tg, gx0, gy0, gy1, gx1,
    cb, tb, bx0, by0, by1, bx1, tc, cx0, cy0, cy1, cx1, bfull, bturn,
    co, to, ox0, oy0, oy1, ox1, oall,
    m1, m2, mb, cm, tm, mx0, my0, my1, mx1, mfin,
    gall, lfull, stat, smate, dfull, kbuf,
    rall, rpick, rmate, sall, spick, sgot,
    usend, urecv, ylsend, ylrecv, ufin, uall,
    ssem, rsem, asend, arecv, lsem,
):
    net = Net(ssem, rsem)
    x, yh, c, yl, z = net.x, net.yh, net.c, net.yl, net.z
    dp = lax.axis_index("dp")
    home = x * 2 + yh
    oc = 1 - c

    barrier = pltpu.get_barrier_semaphore()
    others = [
        net.at(x=lax.rem(x + i, NX), yh=lax.rem(yh + j, 2), c=lax.rem(c + k, 2))
        for i in range(4) for j in range(2) for k in range(2) if (i, j, k) != (0, 0, 0)
    ]
    others += [net.at(yl=1 - yl), net.at(z=lax.rem(z + 1, NZ)), net.at(z=lax.rem(z + NZ - 1, NZ))]
    for device in others:
        pl.semaphore_signal(barrier, inc=1, device_id=device, device_id_type=MESH)

    def pick(b):
        local = slot_ref[b] - (dp - c) * 2
        inside = (local >= 0) & (local < 4)
        return jnp.where(inside, lax.rem(local + 2 * c + 4, 4), 4)

    def block_of(group, s):
        found = 8
        for b in range(NB):
            found = jnp.where(slot_ref[b] == group * 2 + s, b, found)
        return found

    half_lanes = pl.ds(pl.multiple_of(c * 512, 512), 512)
    other_lanes = pl.ds(pl.multiple_of(oc * 512, 512), 512)
    half_b = pl.ds(pl.multiple_of(c * 1024, 1024), 1024)
    other_b = pl.ds(pl.multiple_of(oc * 1024, 1024), 1024)
    half_o = pl.ds(pl.multiple_of(c * 32, 32), 32)
    other_o = pl.ds(pl.multiple_of(oc * 32, 32), 32)

    def load(i, src, dst):
        copy = pltpu.make_async_copy(src, dst, lsem.at[i])
        copy.start()
        return copy

    load_o = load(0, o_ref.at[:, half_o, :], co.at[pl.ds(0, 2)])
    load_b = load(1, b_ref.at[:, half_b, :], cb.at[pl.ds(0, 2)])
    load_a = load(2, a_ref, acts)
    load_g = load(3, g_ref, cot)
    load_m = [load(4, m1_ref, m1), load(5, m2_ref, m2)]
    cb[4] = jnp.zeros_like(cb[4])
    co[4] = jnp.zeros_like(co[4])
    cm[4] = jnp.zeros_like(cm[4])
    pl.semaphore_wait(barrier, len(others))

    ocopy = net.mate(o_ref.at[:, other_o, :], co.at[pl.ds(2, 2)])
    bcopy = net.mate(b_ref.at[:, other_b, :], cb.at[pl.ds(2, 2)])

    def chooser(chunks, held, first=0):
        def body(b, carry):
            chunks[b // 2, b % 2] = held[pick(b), pl.ds(first, chunks.shape[2]), :]
            return carry

        lax.fori_loop(0, NB, body, 0)

    mine = gall.at[yl, z]

    def statistic(a, b):
        at = pl.multiple_of((a * NZ + b) * 128, 128)
        stat[:, pl.ds(at, 128)] = nt(mine[...], gall[a, b])

    right = Scatter(net, to, (ox0, oy0, oy1, ox1), oall.at[yl, z, c], BF, 16)
    head_b = pl.ds(pl.multiple_of(c * 1024, 128), 384)
    tail_b = pl.ds(pl.multiple_of(c * 1024 + 384, 128), 640)
    left = Scatter(net, tb, (bx0, by0, by1, bx1), bfull.at[head_b], BF, 64)
    rest = Scatter(net, tc, (cx0, cy0, cy1, cx1), bfull.at[tail_b], BF, 64)
    moments = Scatter(net, tm, (mx0, my0, my1, mx1), mfin, BF, 32)
    grads = Scatter(net, tg, (gx0, gy0, gy1, gx1), gall.at[yl, z], F32, 32)
    oring = Ring(net, lambda a, b, p: oall.at[a, b, c], 1, lambda a, b: None)
    gring = Ring(net, lambda a, b, p: gall.at[a, b, pl.ds(p * 64, 64), :], 2, statistic)

    load_a.wait()
    turned[...] = acts[...].T
    load_o.wait()
    ocopy.wait_recv()
    chooser(to, co)
    right.start()
    load_b.wait()
    bcopy.wait_recv()
    chooser(tb, cb)
    left.start()
    load_g.wait()
    of_block = lax.broadcasted_iota(jnp.int32, (128, 2048), 1) % NB

    def product(pair, lanes):
        rows = [
            jnp.where(of_block == 2 * pair + i, turned[...], jnp.zeros((), BF)) for i in range(2)
        ]
        return nn(jnp.concatenate(rows, axis=0), cot[:, lanes]).reshape(2, 128, 512)

    pcopies = []
    for pair in range(4):
        psend[pair] = product(pair, other_lanes).astype(BF)
        pcopies.append(net.mate(psend.at[pair], prec.at[pair]))
    for pair in range(4):
        own = product(pair, half_lanes)
        pcopies[pair].wait_recv()
        tg[pair] = (own + prec[pair].astype(F32)).astype(BF)
        if pair == 1:
            right.middle()
    grads.start()

    right.finish()
    oring.start()
    for copy in load_m:
        copy.wait()
    for s in range(2):
        mb[s, 0:128, :] = m1[s].astype(BF)
        mb[s, 128:256, :] = m2[s].astype(BF)
    mcopy = net.mate(mb.at[:, :, other_lanes], cm.at[pl.ds(2, 2)])
    for s in range(2):
        cm[s] = mb[s, :, half_lanes]
    chooser(tc, cb, 384)
    oring.own(1)
    mcopy.wait_recv()
    chooser(tm, cm)
    oring.own(2)

    grads.middle()
    left.middle()
    rest.start_x()
    oring.mate(0)
    oring.own(3)
    grads.finish()
    gring.start()
    moments.start_x()
    oring.mate(1)
    gring.own(1)
    gring.mate(0)
    rest.start_y()
    moments.start_y()
    left.finish()
    gring.own(2)
    oring.mate(2)
    gring.mate(1)
    oring.mate(3)
    gring.own(3)
    rest.middle()
    gring.mate(2)
    oring.finish()
    omate = net.mate(oall.at[:, :, c], oall.at[:, :, c])
    gring.mate(3)
    moments.middle()
    rest.finish()
    bmate = net.mate(bfull.at[half_b], bfull.at[half_b])
    bmate.wait_recv()
    bturn[...] = bfull[...].T
    gring.finish()
    mine_s = pl.ds(pl.multiple_of(c * 64, 64), 64)
    other_s = pl.ds(pl.multiple_of(oc * 64, 64), 64)
    cstat = net.mate(stat.at[other_s, :], smate)

    lfull[:, half_lanes] = nn(bturn[...], gall[...].reshape(2048, 512)).astype(BF)
    lmate = net.mate(lfull.at[:, half_lanes], lfull.at[:, half_lanes])
    cstat.wait_recv()
    sall[x, yh] = (stat[mine_s, :] + smate[...]).astype(BF)
    sspread = Spread(net, sall)
    sspread.start()
    lmate.wait_recv()
    omate.wait_recv()

    basis = oall[:, :, :, :, half_lanes].reshape(1024, 512)
    rotated = nn(lfull[...], basis)
    rall[x, yh] = rotated.astype(BF)
    moments.finish()
    rspread = Spread(net, rall)
    rspread.start()
    first = 0.9 * mfin[0:128, :].astype(F32) + 0.1 * rotated
    second = 0.95 * mfin[128:256, :].astype(F32) + 0.05 * rotated * rotated
    dfull[:, half_lanes] = (first / jnp.sqrt(second)).astype(BF)
    dmate = net.mate(dfull.at[:, half_lanes], dfull.at[:, half_lanes])
    dmate.wait_recv()
    kbuf[...] = nt(dfull[...], oall[c].reshape(512, 1024)).astype(BF)

    def part(zd, yd, p):
        at = pl.multiple_of((yd * NZ + zd) * 128 + p * 64, 64)
        return nn(bfull[pl.ds(at, 64), :], kbuf[...])

    hops = {}
    lines = (1 - yl, yl)

    def ring_hop(way, line, s):
        sign = 1 if way == 0 else -1
        for p in range(2):
            value = part(lax.rem(z + sign * (4 - s) + NZ, NZ), lines[line], p)
            if (way, line, s - 1, p) in hops:
                hops[way, line, s - 1, p].wait_recv()
                value = value + urecv[way, s - 1, line, p].astype(F32)
            usend[way, s, line, p] = value.astype(BF)
            hops[way, line, s, p] = net.send(
                usend.at[way, s, line, p],
                urecv.at[way, s, line, p],
                net.at(z=lax.rem(z + sign + NZ, NZ)),
            )

    zero_r = jnp.zeros((128, 512), BF)
    zero_s = jnp.zeros((64, 2048), BF)

    def chosen(ref, zero, group, s):
        b = block_of(group, s)
        b0 = jnp.minimum(b, NB - 1)
        return jnp.where(b < NB, ref[b0 // 2, b0 % 2], zero)

    mate_group = dp - c + oc

    ring_hop(0, 0, 0)
    ring_hop(1, 1, 0)
    ring_hop(0, 1, 1)
    ring_hop(1, 0, 1)
    sspread.middle()
    ring_hop(0, 0, 1)
    ring_hop(1, 1, 1)
    ring_hop(0, 1, 2)
    ring_hop(1, 0, 2)
    rspread.middle()
    ring_hop(0, 0, 2)
    ring_hop(1, 1, 2)
    ring_hop(1, 0, 3)
    ring_hop(0, 0, 3)
    ring_hop(0, 1, 3)
    ring_hop(1, 1, 3)
    rspread.finish()
    for s in range(2):
        rpick[s] = chosen(rall, zero_r, mate_group, s)
    crm = net.mate(rpick, rmate)

    def final(line, p):
        for way in (0, 1):
            hops[way, line, 3, p].wait_recv()
        here = part(z, lines[line], p)
        return here + urecv[0, 3, line, p].astype(F32) + urecv[1, 3, line, p].astype(F32)

    cyl = []
    for p in range(2):
        ylsend[p] = final(0, p).astype(BF)
        cyl.append(net.send(ylsend.at[p], ylrecv.at[p], net.at(yl=1 - yl)))
    sspread.finish()
    for s in range(2):
        spick[s] = chosen(sall, zero_s, mate_group, s)
    csm = net.mate(spick, sgot)
    for p in range(2):
        own = final(1, p)
        cyl[p].wait_recv()
        ufin[p * 64 : (p + 1) * 64, :] = (own + ylrecv[p].astype(F32)).astype(BF)

    def to_columns(j, k):
        tx, ty = 2 * c + j // 2, j % 2
        here = (tx == x) & (ty == yh) & (k == c)
        src = ufin.at[:, pl.ds(j * 128, 128)]

        def copy():
            return pltpu.make_async_remote_copy(
                src_ref=src,
                dst_ref=uall.at[home],
                send_sem=asend.at[j * 2 + k],
                recv_sem=arecv.at[home],
                device_id=net.at(x=tx, yh=ty, c=k),
                device_id_type=MESH,
            )

        return here, copy

    for j in range(4):
        for k in range(2):
            here, copy = to_columns(j, k)

            @pl.when(jnp.logical_not(here))
            def _(copy=copy):
                copy().start()

            @pl.when(here)
            def _(j=j):
                uall[home] = ufin[:, j * 128 : (j + 1) * 128]

    for s in range(2):
        r_out[s, :, half_lanes] = chosen(rall, zero_r, dp, s)
        s_out[s, mine_s, :] = chosen(sall, zero_s, dp, s)
    crm.wait_recv()
    csm.wait_recv()
    for s in range(2):
        r_out[s, :, other_lanes] = rmate[s]
        s_out[s, other_s, :] = sgot[s]

    for b in range(NB):

        @pl.when(jnp.logical_not((b == home) & (c == x // 2)))
        def _(b=b):
            pltpu.make_async_remote_copy(
                src_ref=uall.at[b],
                dst_ref=uall.at[b],
                send_sem=asend.at[0],
                recv_sem=arecv.at[b],
                device_id=net.at(c=oc),
                device_id_type=MESH,
            ).wait_recv()

        value = uall[b]
        u_out[b] = jnp.where(c == 0, value[:, 0:64], value[:, 64:128]).T

    net.drain()
    for j in range(4):
        for k in range(2):
            here, copy = to_columns(j, k)

            @pl.when(jnp.logical_not(here))
            def _(copy=copy):
                copy().wait_send()


def scatter_bufs(rows, lanes, h=None):
    h = rows // 2 if h is None else h
    return [
        pltpu.VMEM((4, 2, rows, lanes), BF),
        pltpu.VMEM((3, 2, h, lanes), BF),
        pltpu.VMEM((h, lanes), BF),
        pltpu.VMEM((4, rows - h, lanes), BF),
        pltpu.VMEM((3, rows - h, lanes), BF),
    ]


def step(block_slot, acts, cotangent, basis_in, basis_out, moment_first, moment_second):
    vmem = pl.BlockSpec(memory_space=pltpu.VMEM)
    scratch = (
        [
            pltpu.VMEM((2048, 128), BF),
            pltpu.VMEM((2048, 1024), BF),
            pltpu.VMEM((128, 2048), BF),
            pltpu.VMEM((4, 2, 128, 512), BF),
            pltpu.VMEM((4, 2, 128, 512), BF),
        ]
        + scatter_bufs(128, 512)
        + [pltpu.VMEM((5, 1024, 128), BF)] + scatter_bufs(384, 128) + scatter_bufs(640, 128)
        + [pltpu.VMEM((2048, 128), BF), pltpu.VMEM((128, 2048), BF)]
        + [pltpu.VMEM((5, 32, 1024), BF)] + scatter_bufs(32, 1024)
        + [pltpu.VMEM((2, 8, 2, 32, 1024), BF)]
        + [pltpu.VMEM((2, 128, 1024), F32), pltpu.VMEM((2, 128, 1024), F32)]
        + [pltpu.VMEM((2, 256, 1024), BF), pltpu.VMEM((5, 256, 512), BF)] + scatter_bufs(256, 512, 160)
        + [pltpu.VMEM((256, 512), BF)]
        + [
            pltpu.VMEM((2, 8, 128, 512), BF),
            pltpu.VMEM((128, 1024), BF),
            pltpu.VMEM((128, 2048), F32),
            pltpu.VMEM((64, 2048), F32),
            pltpu.VMEM((128, 1024), BF),
            pltpu.VMEM((128, 512), BF),
            pltpu.VMEM((4, 2, 128, 512), BF),
            pltpu.VMEM((2, 128, 512), BF),
            pltpu.VMEM((2, 128, 512), BF),
            pltpu.VMEM((4, 2, 64, 2048), BF),
            pltpu.VMEM((2, 64, 2048), BF),
            pltpu.VMEM((2, 64, 2048), BF),
            pltpu.VMEM((2, 4, 2, 2, 64, 512), BF),
            pltpu.VMEM((2, 4, 2, 2, 64, 512), BF),
            pltpu.VMEM((2, 64, 512), BF),
            pltpu.VMEM((2, 64, 512), BF),
            pltpu.VMEM((128, 512), BF),
            pltpu.VMEM((8, 128, 128), BF),
            pltpu.SemaphoreType.DMA((192,)),
            pltpu.SemaphoreType.DMA((192,)),
            pltpu.SemaphoreType.DMA((8,)),
            pltpu.SemaphoreType.DMA((8,)),
            pltpu.SemaphoreType.DMA((6,)),
        ]
    )
    return pl.pallas_call(
        kernel,
        out_shape=(
            jax.ShapeDtypeStruct((2, 128, 1024), BF),
            jax.ShapeDtypeStruct((2, 128, 2048), BF),
            jax.ShapeDtypeStruct((8, 64, 128), BF),
        ),
        in_specs=[pl.BlockSpec(memory_space=pltpu.SMEM)] + [pl.BlockSpec(memory_space=pl.ANY)] * 6,
        out_specs=(vmem, vmem, vmem),
        scratch_shapes=scratch,
        compiler_params=pltpu.CompilerParams(
            collective_id=0, has_side_effects=True, vmem_limit_bytes=56 << 20
        ),
        name="soap_step",
    )(block_slot, acts, cotangent, basis_in, basis_out, moment_first, moment_second)


def per_device(acts, cotangent, block_slot, basis_in, basis_out, moment_first, moment_second):
    rotated, stat, update = step(
        block_slot,
        acts.reshape(-1, acts.shape[2]),
        cotangent.reshape(-1, cotangent.shape[2]),
        basis_in,
        basis_out,
        moment_first,
        moment_second,
    )
    rotated = rotated.astype(F32)
    new_first = 0.9 * moment_first + 0.1 * rotated
    new_second = 0.95 * moment_second + 0.05 * rotated * rotated
    return (new_first, new_second, stat.astype(F32), jnp.swapaxes(update, 1, 2))


def solution(mesh):
    placed = (
        P("dp", None, "mp"),
        P("dp", None, None),
        P(),
        P("dp", None, "mp"),
        P("dp", "mp", None),
        P("dp", "mp", None),
        P("dp", "mp", None),
    )
    return jax.shard_map(
        per_device,
        mesh=mesh,
        in_specs=placed,
        out_specs=(
            P("dp", "mp", None),
            P("dp", "mp", None),
            P("dp", "mp", None),
            P(None, "mp", "dp"),
        ),
        check_vma=False,
    )
```
